512 devices in a mesh: gx: 32 (over z_lo, y), gy: 4 (over z_hi, core), gz: 4 (over x).
Axes of the slice: x: 4, y: 8, z: 8 (z_hi: 2, z_lo: 4; z = z_hi * 4 + z_lo), core: 2. Of those that a mesh axis runs over, the one named last changes fastest.
Arguments:
- displacement: float32 [3, 768, 128, 512], P(None, 'gx', 'gy', 'gz'), may hold values from -40 to 40, as said below
- density: float32 [768, 128, 512], P('gx', 'gy', 'gz'), may hold values from 0.05 to 1
Outputs:
- sensitivity: float32 [768, 128, 512], P('gx', 'gy', 'gz')
- mean_energy: float32 [], replicated
The draws below stay inside these ranges and needn't reach their ends.
Inputs may be any that keep to these rules, and one draw needn't show every extreme that they name: `displacement`: displacements of the stored nodes.
All inputs are finite; a program needn't handle non-finite values.
Results may differ from the reference program's by a relative error of at most 0.0001.
Values sent between devices are 32-bit elements; how exact they have to be, the bound alone decides.
A program may use at most 64 MiB of HBM per device.

```python
import math
import jax
import jax.numpy as jnp
import numpy as np
from jax import lax

NX = 768
NY = 128
NZ = 512
ELEMENTS = 50331648


def draw_displacement(key, part):
    key = jax.random.fold_in(key, 11)
    first, second, third = jax.random.split(key, 3)
    ramp = 3.0 ** (jnp.arange(NX, dtype=jnp.float32) / NX)
    across_y = jnp.exp(jax.random.uniform(second, (NY,), jnp.float32, 0.0, math.log(3.3)))
    across_z = jnp.exp(jax.random.uniform(third, (NZ,), jnp.float32, 0.0, math.log(3.3)))
    base = jnp.clip(jax.random.normal(first, (3, NX, NY, NZ), jnp.float32), -4.0, 4.0)
    return 0.3 * base * ramp[:, None, None] * across_y[:, None] * across_z


def block_scale(key, shape, cuts, low, top_value):
    def one(axis_at, blocks):
        draws = jax.random.uniform(jax.random.fold_in(jax.random.fold_in(key, 6), axis_at), (blocks,), jnp.float32, low / len(cuts), top_value / len(cuts))
        return jnp.repeat(jnp.exp(draws), shape[axis_at] // blocks).reshape((-1,) + (1,) * (len(shape) - axis_at - 1))

    gain = one(*cuts[0])
    for cut in cuts[1:]:
        gain = gain * one(*cut)
    return gain


def setup_inputs(seed: int = 0) -> dict:
    key_list = jax.random.split(jax.random.key(seed), 3)
    return {
        "displacement": draw_displacement(jax.random.fold_in(key_list[2], 71), 0),
        "density": jnp.clip(0.05 + 0.95 * jax.random.uniform(key_list[1], (NX, NY, NZ), jnp.float32) ** block_scale(key_list[1], (NX, NY, NZ), ((0, 32), (1, 4), (2, 4)), -0.2, 0.2), 0.05, 1.0),
    }


HAT = (1.0, 2.0, 3.0, 2.0, 1.0)

def brick_stiffness():
    ratio = 0.3
    lame_first = ratio / ((1.0 + ratio) * (1.0 - 2.0 * ratio))
    shear = 1.0 / (2.0 * (1.0 + ratio))
    elastic = np.zeros((6, 6))
    elastic[:3, :3] = lame_first
    for index in range(3):
        elastic[index, index] += 2.0 * shear
        elastic[index + 3, index + 3] = shear
    point = 1.0 / np.sqrt(3.0)
    result = np.zeros((24, 24))
    for first in (-point, point):
        for second in (-point, point):
            for third in (-point, point):
                strain_map = np.zeros((6, 24))
                for corner in range(8):
                    signs = [2 * (corner // 4) - 1, 2 * (corner // 2 % 2) - 1, 2 * (corner % 2) - 1]
                    along_x = signs[0] * (1 + signs[1] * second) * (1 + signs[2] * third) / 4.0
                    along_y = signs[1] * (1 + signs[0] * first) * (1 + signs[2] * third) / 4.0
                    along_z = signs[2] * (1 + signs[0] * first) * (1 + signs[1] * second) / 4.0
                    base = 3 * corner
                    strain_map[0, base] = along_x
                    strain_map[1, base + 1] = along_y
                    strain_map[2, base + 2] = along_z
                    strain_map[3, base] = along_y
                    strain_map[3, base + 1] = along_x
                    strain_map[4, base + 1] = along_z
                    strain_map[4, base + 2] = along_y
                    strain_map[5, base] = along_z
                    strain_map[5, base + 2] = along_x
                result += strain_map.T @ elastic @ strain_map / 8.0
    return result

def hat_valid(padded, dim, count):
    total = HAT[0] * lax.slice_in_dim(padded, 0, count, axis=dim)
    for offset in range(1, 5):
        total = total + HAT[offset] * lax.slice_in_dim(padded, offset, offset + count, axis=dim)
    return total

def coverage(count, start, extent):
    positions = start + jnp.arange(count, dtype=jnp.int32)
    total = jnp.zeros((count,), jnp.float32)
    for offset in range(5):
        near = positions + (offset - 2)
        inside = (near >= 0) & (near < extent)
        total = total + jnp.where(inside, jnp.float32(HAT[offset]), jnp.float32(0.0))
    return total

def element_energy(low, high, stiffness):
    rows = low.shape[2] - 1
    depth = low.shape[3]

    def slab(index):
        lows = lax.dynamic_slice_in_dim(low, index, 2, 1)
        highs = lax.dynamic_slice_in_dim(high, index, 2, 1)
        corners = []
        for corner in range(8):
            source = highs if corner % 2 else lows
            shift_y = corner // 2 % 2
            corners.append(source[:, corner // 4, shift_y:shift_y + rows, :])
        vector = jnp.stack(corners, 0).reshape(24, rows * depth)
        image = jnp.dot(stiffness, vector, precision=lax.Precision.HIGHEST)
        return lax.optimization_barrier(jnp.sum(vector * image, 0)).reshape(rows, depth)
    return lax.map(slab, jnp.arange(low.shape[1] - 1, dtype=jnp.int32))

def smooth(field):
    for dim in range(3):
        widths = [(0, 0), (0, 0), (0, 0)]
        widths[dim] = (2, 2)
        field = hat_valid(jnp.pad(field, widths), dim, field.shape[dim])
    return field

def reference(displacement, density):
    stiffness = jnp.asarray(brick_stiffness(), jnp.float32)
    normal = coverage(NX, 0, NX)[:, None, None] * coverage(NY, 0, NY)[None, :, None] * coverage(NZ, 0, NZ)[None, None, :]
    physical = smooth(density) / normal
    padded = jnp.pad(displacement, ((0, 0), (0, 1), (0, 1), (0, 1)))
    energy = element_energy(padded[..., :-1], padded[..., 1:], stiffness)
    mean_energy = jnp.sum(physical ** 3 * energy) / ELEMENTS
    slope = -3.0 * physical ** 2 * energy
    sensitivity = smooth(slope / normal) / mean_energy
    return (sensitivity, mean_energy)
```

```python
import functools
import itertools

import jax
import jax.numpy as jnp
from jax import lax
from jax.experimental import pallas as pl
from jax.experimental.pallas import tpu as pltpu
from jax.sharding import PartitionSpec as P

MESH = pl.DeviceIdType.MESH
F32 = jnp.float32
NX, NY, NZ = 24, 32, 128
ROWS = NX * NY
GROUPS = ROWS // 128
YPAD = 48
NODE_PAD = 40
LAME = 0.3 / (1.3 * 0.4)
SHEAR = 1.0 / 2.6

DIRECTIONS = [d for d in itertools.product((-1, 0, 1), repeat=3) if any(d)]
LOWER = [d for d in DIRECTIONS if max(d) <= 0]


def slot(direction):
    return (direction[0] + 1) * 9 + (direction[1] + 1) * 3 + direction[2] + 1


def lower_slot(direction):
    return -(direction[0] * 4 + direction[1] * 2 + direction[2])


def iota(shape, axis):
    return lax.broadcasted_iota(jnp.int32, shape, axis)


def hat_lanes(v):
    lane = iota(v.shape, v.ndim - 1)
    axis = v.ndim - 1

    def moved(step):
        rolled = pltpu.roll(v, step % NZ, axis)
        return jnp.where(lane >= step if step > 0 else lane < NZ + step, rolled, 0.0)

    return 3.0 * v + 2.0 * (moved(1) + moved(-1)) + (moved(2) + moved(-2))


def across(v, axis, size, step, direction):
    place = iota(v.shape, axis) // step
    count = size // step
    if direction > 0:
        two, one = pltpu.roll(v, 2 * step, axis), pltpu.roll(v, step, axis)
        return jnp.where(place == 0, two + 2.0 * one, jnp.where(place == 1, two, 0.0))
    two, one = pltpu.roll(v, size - 2 * step, axis), pltpu.roll(v, size - step, axis)
    return jnp.where(place == count - 1, two + 2.0 * one, jnp.where(place == count - 2, two, 0.0))


def kernel(sizes, density, displacement, out, total_out, *scratch):
    (field, g, b4, h, acc, rows, corner, nodes, hz, sd, last, energy,
     xs, ys, xys, zs, xzs, yzs, xyzs, xr, yr, xyr, zr, xzr, yzr, xyzr,
     dys, dxys, dzs, dxzs, dyzs, dxyzs, dzr, dxzr, dyzr, dxyzr, m6,
     part, part_in, send_sem, recv_sem, dsend_sem, drecv_sem, load_sem, psend_sem, precv_sem) = scratch
    size_x, size_y, size_z, ring_y = sizes
    gx, gy, gz = (lax.axis_index(a) for a in ("gx", "gy", "gz"))

    def inside(direction):
        ok = []
        for place, step, count in zip((gx, gy, gz), direction, (size_x, size_y, size_z)):
            if step > 0:
                ok.append(place < count - 1)
            elif step < 0:
                ok.append(place > 0)
        return functools.reduce(jnp.logical_and, ok)

    def device(direction):
        return (gx + direction[0], gy + direction[1], gz + direction[2])

    layers_z = size_x // ring_y
    my_y, my_z = lax.rem(gx, ring_y), gx // ring_y + layers_z * (gy // 2)
    my_core = lax.rem(gy, 2)
    count_z = layers_z * (size_y // 2)

    def partner_zc(dz, dc):
        z, c = lax.rem(my_z + dz, count_z), lax.rem(my_core + dc, 2)
        return (lax.rem(z, layers_z) * ring_y + my_y, (z // layers_z) * 2 + c, gz)

    def partner_xy(dx, dy):
        x, y = lax.rem(gz + dx, size_z), lax.rem(my_y + dy, ring_y)
        return ((gx // ring_y) * ring_y + y, gy, x)

    def far_first(counts):
        offs = [o for o in itertools.product(*[range(c) for c in counts]) if any(o)]
        return sorted(offs, key=lambda o: -sum(min(s, c - s) for s, c in zip(o, counts)))

    stages = [
        (partner_zc, far_first((count_z, 2)), my_z * 2 + my_core),
        (partner_xy, far_first((size_z, ring_y)), gz * ring_y + my_y),
    ]

    load_density = pltpu.make_async_copy(density, field.at[pl.ds(2 * NY, ROWS)], load_sem.at[0])
    load_nodes = pltpu.make_async_copy(displacement, nodes.at[:, pl.ds(0, ROWS)], load_sem.at[1])
    load_density.start()
    load_nodes.start()

    zero_row = jnp.zeros((8, NZ), F32)

    def zero(ref):
        ref[...] = jnp.zeros(ref.shape, F32)

    received = {}
    for d in DIRECTIONS:
        sx, sy, sz = ((s + 1) // 2 for s in d)
        kind = tuple(bool(s) for s in d)
        received[d] = {
            (True, False, False): lambda p: (xs.at[p, sx], xr.at[p, sx]),
            (False, True, False): lambda p: (ys.at[p, sy], yr.at[p, sy]),
            (True, True, False): lambda p: (xys.at[p, sx, sy], xyr.at[p, sx, sy]),
            (False, False, True): lambda p: (zs.at[p, sz], zr.at[p, sz]),
            (True, False, True): lambda p: (xzs.at[p, sx, sz], xzr.at[p, sx, sz]),
            (False, True, True): lambda p: (yzs.at[p, sy, sz], yzr.at[p, sy, sz]),
            (True, True, True): lambda p: (xyzs.at[p, sx, sy, sz], xyzr.at[p, sx, sy, sz]),
        }[kind]
        received[d] = [received[d](p) for p in range(2)]
    lower = {
        (-1, 0, 0): (nodes.at[:, pl.ds(0, NY)], nodes.at[:, pl.ds(ROWS, NY)]),
        (0, -1, 0): (dys, nodes.at[:, pl.ds(ROWS + NY, NX)]),
        (-1, -1, 0): (dxys, nodes.at[:, pl.ds(ROWS + NY + NX, 8)]),
        (0, 0, -1): (dzs, dzr),
        (-1, 0, -1): (dxzs, dxzr),
        (0, -1, -1): (dyzs, dyzr),
        (-1, -1, -1): (dxyzs, dxyzr),
    }

    for d in DIRECTIONS:
        @pl.when(jnp.logical_not(inside(tuple(-s for s in d))))
        def _(d=d):
            for p in range(2):
                zero(received[d][p][1])
            if d in lower:
                zero(lower[d][1])

    barrier = pltpu.get_barrier_semaphore()
    waits = 0
    for d in DIRECTIONS:
        @pl.when(inside(d))
        def _(d=d):
            pl.semaphore_signal(barrier, inc=1, device_id=device(d), device_id_type=MESH)
        waits = waits + inside(d).astype(jnp.int32)
    for partner, offsets, _ in stages:
        for o in offsets:
            pl.semaphore_signal(barrier, inc=1, device_id=partner(*o), device_id_type=MESH)
        waits = waits + len(offsets)

    def remote(source, target, send, recv, to):
        return pltpu.make_async_remote_copy(
            src_ref=source, dst_ref=target, send_sem=send, recv_sem=recv, device_id=to, device_id_type=MESH)

    def filter_copy(p, d):
        source, target = received[d][p]
        return remote(source, target, send_sem.at[p, slot(d)], recv_sem.at[p, slot(d)], device(d))

    def lower_copy(d):
        source, target = lower[d]
        return remote(source, target, dsend_sem.at[lower_slot(d)], drecv_sem.at[lower_slot(d)], device(d))

    for margin in (0, NY, (NX + 2) * NY, (NX + 3) * NY):
        field[pl.ds(margin, NY), :] = jnp.zeros((NY, NZ), F32)

    def clear(i, _):
        base = pl.multiple_of(i * YPAD, 16)
        g[pl.ds(base, 8), :] = zero_row
        g[pl.ds(base + 40, 8), :] = zero_row
        return 0

    lax.fori_loop(0, NX, clear, 0)
    for i in range(4):
        b4[pl.ds(i * YPAD, 8), :] = zero_row
        b4[pl.ds(i * YPAD + 40, 8), :] = zero_row
    zero(rows)
    zero(corner)
    zero(m6)

    def hat_rows(ref, base):
        at = [ref[pl.ds(base + 6 + k, NY), :] for k in range(5)]
        return 3.0 * at[2] + 2.0 * (at[1] + at[3]) + (at[0] + at[4])

    def local_filter(p):
        for n, layer in enumerate((0, 1, NX - 2, NX - 1)):
            b4[pl.ds(n * YPAD + 8, NY), :] = field[pl.ds((layer + 2) * NY, NY), :]
        faces = [hat_rows(b4, n * YPAD) for n in range(4)]
        for n in range(4):
            xs[p, n // 2, pl.ds((n % 2) * NY, NY), :] = hat_lanes(faces[n])
        turned = jnp.concatenate(faces, 0).T
        for sz, part_z in enumerate((turned[0:8], turned[120:128])):
            for sx in range(2):
                xzs[p, sx, sz] = across(part_z, 1, 128, 32, 2 * sx - 1)

        def x_pass(i, _):
            at = [field[pl.ds(pl.multiple_of((i + k) * NY, NY), NY), :] for k in range(5)]
            g[pl.ds(pl.multiple_of(i * YPAD, 16) + 8, NY), :] = 3.0 * at[2] + 2.0 * (at[1] + at[3]) + (at[0] + at[4])
            return 0

        lax.fori_loop(0, NX, x_pass, 0)

        for n, row in enumerate((0, 1, NY - 2, NY - 1)):
            edge = g[pl.ds(8 + row, NX, stride=YPAD), :]
            rows[pl.ds(n * 32, NX), :] = edge
            ys[p, n // 2, n % 2] = hat_lanes(edge)
            raw = field[pl.ds(2 * NY + row, NX, stride=NY), :]
            up, down = across(raw[NX - 8:], 0, 8, 1, 1), across(raw[:8], 0, 8, 1, -1)
            corner[pl.ds(n * 32, 8), :] = up
            corner[pl.ds(n * 32 + NX - 8, 8), :] = down
            xys[p, 1, n // 2, n % 2] = hat_lanes(up)
            xys[p, 0, n // 2, n % 2] = hat_lanes(down)
        turned = rows[...].T
        for sz, part_z in enumerate((turned[0:8], turned[120:128])):
            for sy in range(2):
                yzs[p, sy, sz] = across(part_z, 1, 128, 32, 2 * sy - 1)
        turned = corner[...].T
        lane = lax.rem(iota((8, 128), 1), 32)
        for sz, part_z in enumerate((turned[0:8], turned[120:128])):
            for sy in range(2):
                both = across(part_z, 1, 128, 32, 2 * sy - 1)
                xyzs[p, 1, sy, sz] = jnp.where(lane < 8, both, 0.0)
                xyzs[p, 0, sy, sz] = jnp.where(lane < 8, 0.0, both)

        def y_pass(i, _):
            v = hat_rows(g, pl.multiple_of(i * YPAD, 16))
            h[pl.ds(pl.multiple_of(i * NY, NY), NY), :] = v
            acc[pl.ds(pl.multiple_of(i * NY, NY), NY), :] = hat_lanes(v)
            return 0

        lax.fori_loop(0, NX, y_pass, 0)
        for k in range(GROUPS):
            turned = h[pl.ds(k * 128, 128), :].T
            zs[p, 0, :, pl.ds(k * 128, 128)] = turned[0:8]
            zs[p, 1, :, pl.ds(k * 128, 128)] = turned[120:128]

    def send_filter(p):
        for d in DIRECTIONS:
            @pl.when(inside(d))
            def _(d=d):
                filter_copy(p, d).start()

    def add_received(p):
        for d in DIRECTIONS:
            @pl.when(inside(tuple(-s for s in d)))
            def _(d=d):
                filter_copy(p, d).wait_recv()
        def add(layer, v):
            acc[pl.ds(layer * NY, NY), :] = acc[pl.ds(layer * NY, NY), :] + v

        first, second = xr[p, 1, pl.ds(0, NY), :], xr[p, 1, pl.ds(NY, NY), :]
        add(0, first + 2.0 * second)
        add(1, second)
        first, second = xr[p, 0, pl.ds(0, NY), :], xr[p, 0, pl.ds(NY, NY), :]
        add(NX - 2, first)
        add(NX - 1, 2.0 * first + second)
        low = sum([yzr[p, sy, 1] for sy in range(2)] + [xyzr[p, sx, sy, 1] for sx in range(2) for sy in range(2)])
        high = sum([yzr[p, sy, 0] for sy in range(2)] + [xyzr[p, sx, sy, 0] for sx in range(2) for sy in range(2)])
        middle = jnp.zeros((112, 128), F32)
        turned = jnp.concatenate([across(low, 0, 8, 1, 1), middle, across(high, 0, 8, 1, -1)], 0).T
        at = {}
        for sy in range(2):
            for n in range(2):
                center = yr[p, sy, n]
                at[sy, n] = jnp.concatenate(
                    [center[:8] + xyr[p, 1, sy, n], center[8:16], center[16:] + xyr[p, 0, sy, n]], 0)
        for n, (row, v) in enumerate((
                (0, at[1, 0] + 2.0 * at[1, 1]), (1, at[1, 1]), (NY - 2, at[0, 0]), (NY - 1, 2.0 * at[0, 0] + at[0, 1]))):
            place = pl.ds(row, NX, stride=NY)
            acc[place, :] = acc[place, :] + v + turned[n * 32:n * 32 + NX]
        for k in range(GROUPS):
            low, high = zr[p, 1, :, pl.ds(k * 128, 128)], zr[p, 0, :, pl.ds(k * 128, 128)]
            if k == 0:
                low, high = low + xzr[p, 1, 1], high + xzr[p, 1, 0]
            if k == GROUPS - 1:
                low, high = low + xzr[p, 0, 1], high + xzr[p, 0, 0]
            turned = jnp.concatenate([across(low, 0, 8, 1, 1), middle, across(high, 0, 8, 1, -1)], 0).T
            acc[pl.ds(k * 128, 128), :] = acc[pl.ds(k * 128, 128), :] + turned

    load_density.wait()
    local_filter(0)
    load_nodes.wait()

    def first_columns(v):
        lane = iota(v[0].shape, 1)
        return jnp.where(lane == 0, v[0], jnp.where(
            lane == 1, pltpu.roll(v[1], 1, 1), jnp.where(lane == 2, pltpu.roll(v[2], 2, 1), 0.0)))

    for m in range(3):
        dys[m] = nodes[m, pl.ds(0, NX, stride=NY), :]
        dxys[m] = dys[m, pl.ds(0, 8), :]
    for k in range(GROUPS):
        columns = first_columns([nodes[m, pl.ds(k * 128, 128), :] for m in range(3)])
        dzs[:, pl.ds(k * 128, 128)] = columns.T[0:8]
        if k == 0:
            m6[pl.ds(0, NY), :] = columns[:NY]
    m6[pl.ds(NY, NX), :] = first_columns([dys[m] for m in range(3)])
    turned = m6[...].T[0:8]
    lane8 = iota((8, 128), 1)
    dxzs[...] = jnp.where(lane8 < NY, turned, 0.0)
    dyzs[...] = jnp.where(jnp.logical_and(lane8 >= NY, lane8 < NY + NX), turned, 0.0)
    dxyzs[...] = jnp.where(lane8 == NY + NX, pltpu.roll(turned, NY + NX, 1), 0.0)

    pl.semaphore_wait(barrier, waits)
    for d in LOWER:
        @pl.when(inside(d))
        def _(d=d):
            lower_copy(d).start()
    send_filter(0)

    for d in LOWER:
        @pl.when(inside(tuple(-s for s in d)))
        def _(d=d):
            lower_copy(d).wait_recv()
    rest = jnp.zeros((120, 128), F32)
    for k in range(GROUPS + 1):
        if k < GROUPS:
            packed = dzr[:, pl.ds(k * 128, 128)]
        else:
            packed = dxzr[...] + dyzr[...] + dxyzr[...]
        turned = jnp.concatenate([packed, rest], 0).T
        if k < GROUPS:
            hz[pl.ds(k * 128, 128), :] = turned
        else:
            hz[pl.ds(k * 128, 64), :] = turned[:64]

    def z_pass(base):
        halo = hz[pl.ds(base, NY), :]
        lane = iota(halo.shape, 1)
        out = []
        for m in range(3):
            u = nodes[m, pl.ds(base, NY), :]
            t = halo if m == 0 else pltpu.roll(halo, NZ - m, 1)
            up = pltpu.roll(jnp.where(lane == 0, t, u), NZ - 1, 1)
            out += [u + up, up - u]
        return out

    for k, v in enumerate(z_pass(ROWS + NY)):
        last[k] = v

    def z_layer(i, _):
        base = pl.multiple_of(i * NODE_PAD, 8)
        for k, v in enumerate(z_pass(pl.multiple_of(i * NY, NY))):
            sd[k, pl.ds(base, NY), :] = v
            sd[k, pl.ds(base + NY, 1), :] = last[k, pl.ds(i, 1), :]
        return 0

    lax.fori_loop(0, NX + 1, z_layer, 0)

    def yz_terms(i, t):
        base = pl.multiple_of(i * NODE_PAD, 8) + 8 * t
        out = []
        for k in range(6):
            here, above = sd[k, pl.ds(base, 8), :], sd[k, pl.ds(base + 1, 8), :]
            out += [here + above, above - here]
        return out

    square = lambda v: v * v

    for t in range(NY // 8):
        def element(i, before, t=t):
            now = yz_terms(i, t)
            w = []
            for m in range(3):
                (a0, a1, a2, a3), (b0, b1, b2, b3) = now[4 * m:4 * m + 4], before[4 * m:4 * m + 4]
                w.append({100: a0 - b0, 110: a1 - b1, 101: a2 - b2, 111: a3 - b3,
                          10: a1 + b1, 1: a2 + b2, 11: a3 + b3})
            u, v, z = w
            total = (LAME / 16) * square(u[100] + v[10] + z[1])
            total += (LAME / 48) * (square(v[110] + z[101]) + square(u[110] + z[11]) + square(u[101] + v[11]))
            total += (SHEAR / 8) * (square(u[100]) + square(v[10]) + square(z[1]))
            total += (SHEAR / 16) * (
                (square(u[110]) + square(u[101]) + square(v[110])) + (square(v[11]) + square(z[101]) + square(z[11]))
                + (square(u[10] + v[100]) + square(v[1] + z[10]) + square(u[1] + z[100])))
            total += (SHEAR / 48) * (square(u[11] + v[101]) + square(v[101] + z[110]) + square(u[11] + z[110]))
            total += ((LAME + 4 * SHEAR) / 144) * (square(u[111]) + square(v[111]) + square(z[111]))
            energy[pl.ds(pl.multiple_of((i - 1) * NY, NY) + 8 * t, 8), :] = total
            return tuple(now)

        lax.fori_loop(1, NX + 1, element, tuple(yz_terms(0, t)))

    add_received(0)

    def inverse_cover(index, extent):
        end = extent - 1
        return jnp.where(jnp.logical_or(index == 0, index == end), 1.0 / 6.0, jnp.where(
            jnp.logical_or(index == 1, index == end - 1), 1.0 / 8.0, 1.0 / 9.0)).astype(F32)

    inverse_yz = inverse_cover(iota((NY, NZ), 0) + gy * NY, NY * size_y) * inverse_cover(
        iota((NY, NZ), 1) + gz * NZ, NZ * size_z)

    def weigh(i, total):
        base = pl.multiple_of(i * NY, NY)
        inverse = inverse_yz * inverse_cover(gx * NX + i, NX * size_x)
        physical = acc[pl.ds(base, NY), :] * inverse
        product = physical * physical * energy[pl.ds(base, NY), :]
        field[pl.ds(base + 2 * NY, NY), :] = -3.0 * product * inverse
        return total + physical * product

    total = lax.fori_loop(0, NX, weigh, jnp.zeros((NY, NZ), F32))
    total = jnp.sum(total, axis=0, keepdims=True)

    def send_total(s, value):
        partner, offsets, mine = stages[s]
        part[s] = value
        part_in[s, mine] = value
        for o in offsets:
            remote(part.at[s], part_in.at[s, mine], psend_sem.at[s], precv_sem.at[s], partner(*o)).start()

    def total_wait(s, sem):
        n = len(stages[s][1])
        whole = part_in.at[s, pl.ds(0, n)]
        pltpu.make_async_copy(whole, whole, sem.at[s]).wait()

    def receive_total(s):
        total_wait(s, precv_sem)
        return jnp.sum(part_in[s, 0:len(stages[s][1]) + 1], axis=0)

    send_total(0, total)
    local_filter(1)
    send_filter(1)
    send_total(1, receive_total(0))
    add_received(1)
    out[...] = acc[...]
    total = receive_total(1)
    total_out[...] = jnp.broadcast_to(jnp.sum(total, axis=1, keepdims=True), (8, 128))

    for d in DIRECTIONS:
        @pl.when(inside(d))
        def _(d=d):
            for p in range(2):
                filter_copy(p, d).wait_send()
            if d in lower:
                lower_copy(d).wait_send()
    for s in range(2):
        total_wait(s, psend_sem)


def exchange(mesh, density, displacement):
    sizes = (mesh.shape["gx"], mesh.shape["gy"], mesh.shape["gz"], min(8, mesh.shape["gx"]))
    vmem = lambda *shape: pltpu.VMEM(shape, F32)
    partners = max(sizes[0] // sizes[3] * sizes[1], sizes[3] * sizes[2])
    scratch = [
        vmem((NX + 4) * NY, NZ), vmem(NX * YPAD, NZ), vmem(4 * YPAD, NZ), vmem(ROWS, NZ), vmem(ROWS, NZ),
        vmem(128, NZ), vmem(128, NZ), vmem(3, ROWS + 2 * NY, NZ), vmem(ROWS + 2 * NY, NZ),
        vmem(6, (NX + 1) * NODE_PAD, NZ), vmem(6, NY, NZ), vmem(ROWS, NZ)]
    filters = [vmem(2, 2, 2 * NY, NZ), vmem(2, 2, 2, NX, NZ), vmem(2, 2, 2, 2, 8, NZ), vmem(2, 2, 8, ROWS),
               vmem(2, 2, 2, 8, 128), vmem(2, 2, 2, 8, 128), vmem(2, 2, 2, 2, 8, 128)]
    scratch += filters + filters
    scratch += [vmem(3, NX, NZ), vmem(3, 8, NZ), vmem(8, ROWS), vmem(8, 128), vmem(8, 128), vmem(8, 128),
                vmem(8, ROWS), vmem(8, 128), vmem(8, 128), vmem(8, 128), vmem(128, 128)]
    scratch += [vmem(2, 1, 128), vmem(2, partners, 1, 128)]
    dma = pltpu.SemaphoreType.DMA
    scratch += [dma((2, 27)), dma((2, 27)), dma((8,)), dma((8,)), dma((2,)), dma((2,)), dma((2,))]
    return pl.pallas_call(
        functools.partial(kernel, sizes),
        out_shape=[jax.ShapeDtypeStruct((ROWS, NZ), F32), jax.ShapeDtypeStruct((8, 128), F32)],
        in_specs=[pl.BlockSpec(memory_space=pl.ANY)] * 2,
        out_specs=[pl.BlockSpec(memory_space=pltpu.VMEM)] * 2,
        scratch_shapes=scratch,
        compiler_params=pltpu.CompilerParams(
            collective_id=0, has_side_effects=True, vmem_limit_bytes=40 * 2**20),
        cost_estimate=pl.CostEstimate(flops=20_000_000, bytes_accessed=2_000_000, transcendentals=0),
    )(density, displacement)


def scale_kernel(elements, field, total, out, mean_out):
    mean = total[0:1, :] / elements
    out[...] = field[...] / mean
    mean_out[...] = mean[:, 0:1]


def solution(mesh):
    def shards(displacement, density):
        filtered, total = exchange(mesh, density.reshape(ROWS, NZ), displacement.reshape(3, ROWS, NZ))
        sensitivity, mean = pl.pallas_call(
            functools.partial(scale_kernel, float(ROWS * NZ * mesh.size)),
            out_shape=[jax.ShapeDtypeStruct((ROWS, NZ), F32), jax.ShapeDtypeStruct((1, 1), F32)],
        )(filtered, total)
        return sensitivity.reshape(NX, NY, NZ), mean.reshape(())

    return jax.shard_map(
        shards,
        mesh=mesh,
        in_specs=(P(None, "gx", "gy", "gz"), P("gx", "gy", "gz")),
        out_specs=(P("gx", "gy", "gz"), P()),
        check_vma=False,
    )
```

```python
import functools
import itertools

import jax
import jax.numpy as jnp
from jax import lax
from jax.experimental import pallas as pl
from jax.experimental.pallas import tpu as pltpu
from jax.sharding import PartitionSpec as P

MESH = pl.DeviceIdType.MESH
F32 = jnp.float32
NX, NY, NZ = 24, 32, 128
ROWS = NX * NY
GROUPS = ROWS // 128
YPAD = 48
NODE_PAD = 40
PARTS = 4
LAME = 0.3 / (1.3 * 0.4)
SHEAR = 1.0 / 2.6

DIRECTIONS = sorted((d for d in itertools.product((-1, 0, 1), repeat=3) if any(d)), key=lambda d: (not d[1], sum(map(abs, d))))
LOWER = [d for d in DIRECTIONS if max(d) <= 0]


def slot(direction):
    return (direction[0] + 1) * 9 + (direction[1] + 1) * 3 + direction[2] + 1


def lower_slot(direction):
    return -(direction[0] * 4 + direction[1] * 2 + direction[2])


def iota(shape, axis):
    return lax.broadcasted_iota(jnp.int32, shape, axis)


def hat_lanes(v):
    lane = iota(v.shape, v.ndim - 1)
    axis = v.ndim - 1

    def moved(step):
        rolled = pltpu.roll(v, step % NZ, axis)
        return jnp.where(lane >= step if step > 0 else lane < NZ + step, rolled, 0.0)

    return 3.0 * v + 2.0 * (moved(1) + moved(-1)) + (moved(2) + moved(-2))


def across(v, axis, size, step, direction):
    place = iota(v.shape, axis) // step
    count = size // step
    if direction > 0:
        two, one = pltpu.roll(v, 2 * step, axis), pltpu.roll(v, step, axis)
        return jnp.where(place == 0, two + 2.0 * one, jnp.where(place == 1, two, 0.0))
    two, one = pltpu.roll(v, size - 2 * step, axis), pltpu.roll(v, size - step, axis)
    return jnp.where(place == count - 1, two + 2.0 * one, jnp.where(place == count - 2, two, 0.0))


def kernel(sizes, density, displacement, out, total_out, *scratch):
    (field, g, b4, acc, rows, corner, nodes, sd, energy,
     xs, ys, xys, zs, xzs, yzs, xyzs, xr, yr, xyr, zr, xzr, yzr, xyzr,
     dys, dxys, dzs, dxzs, dyzs, dxyzs, dzr, dxzr, dyzr, dxyzr, m6,
     part, part_in, send_sem, recv_sem, dsend_sem, drecv_sem, load_sem, psend_sem, precv_sem) = scratch
    size_x, size_y, size_z, ring_y = sizes
    gx, gy, gz = (lax.axis_index(a) for a in ("gx", "gy", "gz"))

    def inside(direction):
        ok = []
        for place, step, count in zip((gx, gy, gz), direction, (size_x, size_y, size_z)):
            if step > 0:
                ok.append(place < count - 1)
            elif step < 0:
                ok.append(place > 0)
        return functools.reduce(jnp.logical_and, ok)

    def device(direction):
        return (gx + direction[0], gy + direction[1], gz + direction[2])

    layers_z = size_x // ring_y
    my_y, my_z = lax.rem(gx, ring_y), gx // ring_y + layers_z * (gy // 2)
    my_core = lax.rem(gy, 2)
    count_z = layers_z * (size_y // 2)

    def partner_zc(dz, dc):
        z, c = lax.rem(my_z + dz, count_z), lax.rem(my_core + dc, 2)
        return (lax.rem(z, layers_z) * ring_y + my_y, (z // layers_z) * 2 + c, gz)

    def partner_xy(dx, dy):
        x, y = lax.rem(gz + dx, size_z), lax.rem(my_y + dy, ring_y)
        return ((gx // ring_y) * ring_y + y, gy, x)

    def far_first(counts):
        offs = [o for o in itertools.product(*[range(c) for c in counts]) if any(o)]
        return sorted(offs, key=lambda o: -sum(min(s, c - s) for s, c in zip(o, counts)))

    stages = [
        (partner_zc, far_first((count_z, 2)), my_z * 2 + my_core),
        (partner_xy, far_first((size_z, ring_y)), gz * ring_y + my_y),
    ]

    load_density = pltpu.make_async_copy(density, field.at[pl.ds(2 * NY, ROWS)], load_sem.at[0])
    load_nodes = pltpu.make_async_copy(displacement, nodes.at[:, pl.ds(0, ROWS)], load_sem.at[1])
    load_density.start()
    load_nodes.start()

    barrier = pltpu.get_barrier_semaphore()
    waits = 0
    for partner, offsets, _ in stages:
        for o in offsets:
            pl.semaphore_signal(barrier, inc=1, device_id=partner(*o), device_id_type=MESH)
        waits = waits + len(offsets)
        if partner is partner_zc:
            for d in DIRECTIONS:
                @pl.when(inside(d))
                def _(d=d):
                    pl.semaphore_signal(barrier, inc=1, device_id=device(d), device_id_type=MESH)
                waits = waits + inside(d).astype(jnp.int32)

    zero_row = jnp.zeros((8, NZ), F32)

    def zero(ref):
        ref[...] = jnp.zeros(ref.shape, F32)

    received = {}
    for d in DIRECTIONS:
        sx, sy, sz = ((s + 1) // 2 for s in d)
        kind = tuple(bool(s) for s in d)
        received[d] = {
            (True, False, False): lambda p: (xs.at[p, sx], xr.at[p, sx]),
            (False, True, False): lambda p: (ys.at[p, sy], yr.at[p, sy]),
            (True, True, False): lambda p: (xys.at[p, sx, sy], xyr.at[p, sx, sy]),
            (False, False, True): lambda p: (zs.at[p, sz], zr.at[p, sz]),
            (True, False, True): lambda p: (xzs.at[p, sx, sz], xzr.at[p, sx, sz]),
            (False, True, True): lambda p: (yzs.at[p, sy, sz], yzr.at[p, sy, sz]),
            (True, True, True): lambda p: (xyzs.at[p, sx, sy, sz], xyzr.at[p, sx, sy, sz]),
        }[kind]
        received[d] = [received[d](p) for p in range(2)]
    lower = {
        (-1, 0, 0): (nodes.at[:, pl.ds(0, NY)], nodes.at[:, pl.ds(ROWS, NY)]),
        (0, -1, 0): (dys, nodes.at[:, pl.ds(ROWS + NY, NX)]),
        (-1, -1, 0): (dxys, nodes.at[:, pl.ds(ROWS + NY + NX, 8)]),
        (0, 0, -1): (dzs, dzr),
        (-1, 0, -1): (dxzs, dxzr),
        (0, -1, -1): (dyzs, dyzr),
        (-1, -1, -1): (dxyzs, dxyzr),
    }

    for d in DIRECTIONS:
        @pl.when(jnp.logical_not(inside(tuple(-s for s in d))))
        def _(d=d):
            for p in range(2):
                zero(received[d][p][1])
            if d in lower:
                zero(lower[d][1])

    def remote(source, target, send, recv, to):
        return pltpu.make_async_remote_copy(
            src_ref=source, dst_ref=target, send_sem=send, recv_sem=recv, device_id=to, device_id_type=MESH)

    def filter_copy(p, d):
        source, target = received[d][p]
        return remote(source, target, send_sem.at[p, slot(d)], recv_sem.at[p, slot(d)], device(d))

    def lower_copy(d):
        source, target = lower[d]
        return remote(source, target, dsend_sem.at[lower_slot(d)], drecv_sem.at[lower_slot(d)], device(d))

    for margin in (0, NY, (NX + 2) * NY, (NX + 3) * NY):
        field[pl.ds(margin, NY), :] = jnp.zeros((NY, NZ), F32)

    for i in range(NX):
        g[pl.ds(i * YPAD, 8), :] = zero_row
        g[pl.ds(i * YPAD + 40, 8), :] = zero_row
    for i in range(4):
        b4[pl.ds(i * YPAD, 8), :] = zero_row
        b4[pl.ds(i * YPAD + 40, 8), :] = zero_row
    zero(rows)
    zero(corner)
    zero(m6)

    middle = jnp.zeros((112, 128), F32)

    def hat_rows(ref, base):
        at = [ref[pl.ds(base + 6 + k, NY), :] for k in range(5)]
        return 3.0 * at[2] + 2.0 * (at[1] + at[3]) + (at[0] + at[4])

    def local_filter(p, ref):
        for n, layer in enumerate((0, 1, NX - 2, NX - 1)):
            b4[pl.ds(n * YPAD + 8, NY), :] = field[pl.ds((layer + 2) * NY, NY), :]
        faces = [hat_rows(b4, n * YPAD) for n in range(4)]
        for n in range(4):
            xs[p, n // 2, pl.ds((n % 2) * NY, NY), :] = hat_lanes(faces[n])
        turned = jnp.concatenate(faces, 0).T
        for sz, part_z in enumerate((turned[0:8], turned[120:128])):
            for sx in range(2):
                xzs[p, sx, sz] = across(part_z, 1, 128, 32, 2 * sx - 1)

        for t in range(NY // 8):
            at = [field[pl.ds(i * NY + 8 * t, 8), :] for i in range(NX + 4)]
            for i in range(NX):
                g[pl.ds(i * YPAD + 8 + 8 * t, 8), :] = (
                    3.0 * at[i + 2] + 2.0 * (at[i + 1] + at[i + 3]) + (at[i] + at[i + 4]))

        for n, row in enumerate((0, 1, NY - 2, NY - 1)):
            edge = g[pl.ds(8 + row, NX, stride=YPAD), :]
            rows[pl.ds(n * 32, NX), :] = edge
            ys[p, n // 2, n % 2] = hat_lanes(edge)
            raw = field[pl.ds(2 * NY + row, NX, stride=NY), :]
            up, down = across(raw[NX - 8:], 0, 8, 1, 1), across(raw[:8], 0, 8, 1, -1)
            corner[pl.ds(n * 32, 8), :] = up
            corner[pl.ds(n * 32 + NX - 8, 8), :] = down
            xys[p, 1, n // 2, n % 2] = hat_lanes(up)
            xys[p, 0, n // 2, n % 2] = hat_lanes(down)
        turned = rows[...].T
        for sz, part_z in enumerate((turned[0:8], turned[120:128])):
            for sy in range(2):
                yzs[p, sy, sz] = across(part_z, 1, 128, 32, 2 * sy - 1)
        turned = corner[...].T
        lane = lax.rem(iota((8, 128), 1), 32)
        for sz, part_z in enumerate((turned[0:8], turned[120:128])):
            for sy in range(2):
                both = across(part_z, 1, 128, 32, 2 * sy - 1)
                xyzs[p, 1, sy, sz] = jnp.where(lane < 8, both, 0.0)
                xyzs[p, 0, sy, sz] = jnp.where(lane < 8, 0.0, both)

        for k in range(GROUPS):
            v = jnp.concatenate([hat_rows(g, (4 * k + n) * YPAD) for n in range(4)], 0)
            ref[pl.ds(k * 128, 128), :] = hat_lanes(v)
            turned = v.T
            zs[p, 0, :, pl.ds(k * 128, 128)] = turned[0:8]
            zs[p, 1, :, pl.ds(k * 128, 128)] = turned[120:128]

    def send_filter(p):
        for d in DIRECTIONS:
            @pl.when(inside(d))
            def _(d=d):
                filter_copy(p, d).start()

    def wait_received(p, along_y):
        for d in DIRECTIONS:
            if bool(d[1]) == along_y:
                @pl.when(inside(tuple(-s for s in d)))
                def _(d=d):
                    filter_copy(p, d).wait_recv()

    def add_xz(p, acc):
        wait_received(p, False)
        def add(layer, v):
            acc[pl.ds(layer * NY, NY), :] = acc[pl.ds(layer * NY, NY), :] + v

        first, second = xr[p, 1, pl.ds(0, NY), :], xr[p, 1, pl.ds(NY, NY), :]
        add(0, first + 2.0 * second)
        add(1, second)
        first, second = xr[p, 0, pl.ds(0, NY), :], xr[p, 0, pl.ds(NY, NY), :]
        add(NX - 2, first)
        add(NX - 1, 2.0 * first + second)
        for k in range(GROUPS):
            low, high = zr[p, 1, :, pl.ds(k * 128, 128)], zr[p, 0, :, pl.ds(k * 128, 128)]
            if k == 0:
                low, high = low + xzr[p, 1, 1], high + xzr[p, 1, 0]
            if k == GROUPS - 1:
                low, high = low + xzr[p, 0, 1], high + xzr[p, 0, 0]
            turned = jnp.concatenate([across(low, 0, 8, 1, 1), middle, across(high, 0, 8, 1, -1)], 0).T
            acc[pl.ds(k * 128, 128), :] = acc[pl.ds(k * 128, 128), :] + turned

    def add_y(p, acc):
        wait_received(p, True)
        low = sum([yzr[p, sy, 1] for sy in range(2)] + [xyzr[p, sx, sy, 1] for sx in range(2) for sy in range(2)])
        high = sum([yzr[p, sy, 0] for sy in range(2)] + [xyzr[p, sx, sy, 0] for sx in range(2) for sy in range(2)])
        turned = jnp.concatenate([across(low, 0, 8, 1, 1), middle, across(high, 0, 8, 1, -1)], 0).T
        at = {}
        for sy in range(2):
            for n in range(2):
                center = yr[p, sy, n]
                at[sy, n] = jnp.concatenate(
                    [center[:8] + xyr[p, 1, sy, n], center[8:16], center[16:] + xyr[p, 0, sy, n]], 0)
        for n, (row, v) in enumerate((
                (0, at[1, 0] + 2.0 * at[1, 1]), (1, at[1, 1]), (NY - 2, at[0, 0]), (NY - 1, 2.0 * at[0, 0] + at[0, 1]))):
            place = pl.ds(row, NX, stride=NY)
            acc[place, :] = acc[place, :] + v + turned[n * 32:n * 32 + NX]

    load_density.wait()
    local_filter(0, acc)
    load_nodes.wait()

    def first_columns(v):
        lane = iota(v[0].shape, 1)
        return jnp.where(lane == 0, v[0], jnp.where(
            lane == 1, pltpu.roll(v[1], 1, 1), jnp.where(lane == 2, pltpu.roll(v[2], 2, 1), 0.0)))

    for m in range(3):
        dys[m] = nodes[m, pl.ds(0, NX, stride=NY), :]
        dxys[m] = dys[m, pl.ds(0, 8), :]
    for k in range(GROUPS):
        columns = first_columns([nodes[m, pl.ds(k * 128, 128), :] for m in range(3)])
        dzs[:, pl.ds(k * 128, 128)] = columns.T[0:8]
        if k == 0:
            m6[pl.ds(0, NY), :] = columns[:NY]
    m6[pl.ds(NY, NX), :] = first_columns([dys[m] for m in range(3)])
    turned = m6[...].T[0:8]
    lane8 = iota((8, 128), 1)
    dxzs[...] = jnp.where(lane8 < NY, turned, 0.0)
    dyzs[...] = jnp.where(jnp.logical_and(lane8 >= NY, lane8 < NY + NX), turned, 0.0)
    dxyzs[...] = jnp.where(lane8 == NY + NX, pltpu.roll(turned, NY + NX, 1), 0.0)

    pl.semaphore_wait(barrier, waits)
    for d in LOWER:
        @pl.when(inside(d))
        def _(d=d):
            lower_copy(d).start()
    send_filter(0)

    def wait_lower(along_y):
        for d in LOWER:
            if bool(d[1]) == along_y:
                @pl.when(inside(tuple(-s for s in d)))
                def _(d=d):
                    lower_copy(d).wait_recv()

    rest = jnp.zeros((120, 128), F32)

    def z_pass(base, count, packed):
        halo = jnp.concatenate([packed, rest], 0).T[:count]
        lane = iota(halo.shape, 1)
        out = []
        for m in range(3):
            u = nodes[m, pl.ds(base, count), :]
            up = jnp.where(lane == NZ - 1, pltpu.roll(halo, NZ - 1 - m, 1), pltpu.roll(u, NZ - 1, 1))
            out += [u + up, up - u]
        return out

    wait_lower(False)
    for k in range(GROUPS):
        for n, v in enumerate(z_pass(k * 128, 128, dzr[:, pl.ds(k * 128, 128)])):
            for i in range(4):
                sd[n, pl.ds((4 * k + i) * NODE_PAD, NY), :] = v[i * NY:(i + 1) * NY]
    for n, v in enumerate(z_pass(ROWS, NY, dxzr[...])):
        sd[n, pl.ds(NX * NODE_PAD, NY), :] = v

    def yz_terms(i, t):
        base = pl.multiple_of(i * NODE_PAD, 8) + 8 * t
        out = []
        for k in range(6):
            here, above = sd[k, pl.ds(base, 8), :], sd[k, pl.ds(base + 1, 8), :]
            out += [here + above, above - here]
        return out

    square = lambda v: v * v

    def energies(t):
        def element(i, before):
            now = yz_terms(i, t)
            w = []
            for m in range(3):
                (a0, a1, a2, a3), (b0, b1, b2, b3) = now[4 * m:4 * m + 4], before[4 * m:4 * m + 4]
                w.append({100: a0 - b0, 110: a1 - b1, 101: a2 - b2, 111: a3 - b3,
                          10: a1 + b1, 1: a2 + b2, 11: a3 + b3})
            u, v, z = w
            total = (LAME / 16) * square(u[100] + v[10] + z[1])
            total += (LAME / 48) * (square(v[110] + z[101]) + square(u[110] + z[11]) + square(u[101] + v[11]))
            total += (SHEAR / 8) * (square(u[100]) + square(v[10]) + square(z[1]))
            total += (SHEAR / 16) * (
                (square(u[110]) + square(u[101]) + square(v[110])) + (square(v[11]) + square(z[101]) + square(z[11]))
                + (square(u[10] + v[100]) + square(v[1] + z[10]) + square(u[1] + z[100])))
            total += (SHEAR / 48) * (square(u[11] + v[101]) + square(v[101] + z[110]) + square(u[11] + z[110]))
            total += ((LAME + 4 * SHEAR) / 144) * (square(u[111]) + square(v[111]) + square(z[111]))
            energy[pl.ds(pl.multiple_of((i - 1) * NY, NY) + 8 * t, 8), :] = total
            return now

        def pair(n, before):
            return tuple(element(2 * n + 2, element(2 * n + 1, before)))

        lax.fori_loop(0, NX // 2, pair, tuple(yz_terms(0, t)))

    for t in range(NY // 8 - 1):
        energies(t)
    add_xz(0, acc)
    wait_lower(True)
    for n, v in enumerate(z_pass(ROWS + NY, NY, pltpu.roll(dyzr[...] + dxyzr[...], 128 - NY, 1))):
        sd[n, pl.ds(NY, NX + 1, stride=NODE_PAD), :] = v[:NX + 1]
    energies(NY // 8 - 1)

    add_y(0, acc)

    def inverse_cover(index, extent):
        end = extent - 1
        return jnp.where(jnp.logical_or(index == 0, index == end), 1.0 / 6.0, jnp.where(
            jnp.logical_or(index == 1, index == end - 1), 1.0 / 8.0, 1.0 / 9.0)).astype(F32)

    inverse_yz = inverse_cover(iota((NY, NZ), 0) + gy * NY, NY * size_y) * inverse_cover(
        iota((NY, NZ), 1) + gz * NZ, NZ * size_z)

    total = jnp.zeros((NY, NZ), F32)
    for i in range(NX):
        inverse = inverse_yz * inverse_cover(gx * NX + i, NX * size_x)
        physical = acc[pl.ds(i * NY, NY), :] * inverse
        product = physical * physical * energy[pl.ds(i * NY, NY), :]
        field[pl.ds((i + 2) * NY, NY), :] = -3.0 * product * inverse
        total = total + physical * product
    total = jnp.sum(total, axis=0, keepdims=True)

    def send_total(s, value):
        partner, offsets, mine = stages[s]
        part[s] = value
        part_in[s, mine] = value
        for o in offsets:
            remote(part.at[s], part_in.at[s, mine], psend_sem.at[s], precv_sem.at[s], partner(*o)).start()

    def total_wait(s, sem):
        n = len(stages[s][1])
        whole = part_in.at[s, pl.ds(0, n)]
        pltpu.make_async_copy(whole, whole, sem.at[s]).wait()

    def receive_total(s):
        total_wait(s, precv_sem)
        return jnp.sum(part_in[s, 0:len(stages[s][1]) + 1], axis=0)

    send_total(0, total)
    local_filter(1, out)
    send_filter(1)
    send_total(1, receive_total(0))
    add_xz(1, out)
    add_y(1, out)
    total = receive_total(1)
    total_out[...] = jnp.broadcast_to(jnp.sum(total, axis=1, keepdims=True), (8, 128))

    for d in DIRECTIONS:
        @pl.when(inside(d))
        def _(d=d):
            for p in range(2):
                filter_copy(p, d).wait_send()
            if d in lower:
                lower_copy(d).wait_send()
    for s in range(2):
        total_wait(s, psend_sem)


def exchange(mesh, density, displacement):
    sizes = (mesh.shape["gx"], mesh.shape["gy"], mesh.shape["gz"], min(8, mesh.shape["gx"]))
    vmem = lambda *shape: pltpu.VMEM(shape, F32)
    partners = max(sizes[0] // sizes[3] * sizes[1], sizes[3] * sizes[2])
    scratch = [
        vmem((NX + 4) * NY, NZ), vmem(NX * YPAD, NZ), vmem(4 * YPAD, NZ), vmem(ROWS, NZ),
        vmem(128, NZ), vmem(128, NZ), vmem(3, ROWS + 2 * NY, NZ),
        vmem(6, (NX + 1) * NODE_PAD, NZ), vmem(ROWS, NZ)]
    filters = [vmem(2, 2, 2 * NY, NZ), vmem(2, 2, 2, NX, NZ), vmem(2, 2, 2, 2, 8, NZ), vmem(2, 2, 8, ROWS),
               vmem(2, 2, 2, 8, 128), vmem(2, 2, 2, 8, 128), vmem(2, 2, 2, 2, 8, 128)]
    scratch += filters + filters
    scratch += [vmem(3, NX, NZ), vmem(3, 8, NZ), vmem(8, ROWS), vmem(8, 128), vmem(8, 128), vmem(8, 128),
                vmem(8, ROWS), vmem(8, 128), vmem(8, 128), vmem(8, 128), vmem(128, 128)]
    scratch += [vmem(2, 1, 128), vmem(2, partners, 1, 128)]
    dma = pltpu.SemaphoreType.DMA
    scratch += [dma((2, 27)), dma((2, 27)), dma((8,)), dma((8,)), dma((2,)), dma((2,)), dma((2,))]
    return pl.pallas_call(
        functools.partial(kernel, sizes),
        out_shape=[jax.ShapeDtypeStruct((ROWS, NZ), F32), jax.ShapeDtypeStruct((8, 128), F32)],
        in_specs=[pl.BlockSpec(memory_space=pltpu.HBM)] * 2,
        out_specs=[pl.BlockSpec(memory_space=pltpu.VMEM)] * 2,
        scratch_shapes=scratch,
        compiler_params=pltpu.CompilerParams(
            collective_id=0, has_side_effects=True, vmem_limit_bytes=56_000_000),
        cost_estimate=pl.CostEstimate(flops=20_000_000, bytes_accessed=2_000_000, transcendentals=0),
    )(density, displacement)


def scale_kernel(elements, field, total, out, mean_out, scaled, sem):
    mean = total[0:1, :] / elements
    mean_out[...] = mean[:, 0:1]
    inverse = 1.0 / mean
    copies = []
    for n in range(PARTS):
        part = pl.ds(n * (ROWS // PARTS), ROWS // PARTS)
        scaled[part, :] = field[part, :] * inverse
        copies.append(pltpu.make_async_copy(scaled.at[part], out.at[part], sem.at[n]))
        copies[-1].start()
    for copy in copies:
        copy.wait()


def solution(mesh):
    def shards(displacement, density):
        filtered, total = exchange(mesh, density.reshape(ROWS, NZ), displacement.reshape(3, ROWS, NZ))
        sensitivity, mean = pl.pallas_call(
            functools.partial(scale_kernel, float(ROWS * NZ * mesh.size)),
            out_shape=[jax.ShapeDtypeStruct((ROWS, NZ), F32), jax.ShapeDtypeStruct((1, 1), F32)],
            in_specs=[pl.BlockSpec(memory_space=pltpu.VMEM)] * 2,
            out_specs=[pl.BlockSpec(memory_space=pl.ANY), pl.BlockSpec((1, 1), lambda: (0, 0))],
            scratch_shapes=[pltpu.VMEM((ROWS, NZ), F32), pltpu.SemaphoreType.DMA((PARTS,))],
            compiler_params=pltpu.CompilerParams(vmem_limit_bytes=4 * 2**20),
        )(filtered, total)
        return sensitivity.reshape(NX, NY, NZ), mean.reshape(())

    return jax.shard_map(
        shards,
        mesh=mesh,
        in_specs=(P(None, "gx", "gy", "gz"), P("gx", "gy", "gz")),
        out_specs=(P("gx", "gy", "gz"), P()),
        check_vma=False,
    )
```

```python
import functools
import itertools

import jax
import jax.numpy as jnp
from jax import lax
from jax.experimental import pallas as pl
from jax.experimental.pallas import tpu as pltpu
from jax.sharding import PartitionSpec as P

MESH = pl.DeviceIdType.MESH
F32 = jnp.float32
NX, NY, NZ = 24, 32, 128
ROWS = NX * NY
GROUPS = ROWS // 128
YPAD = 48
NODE_PAD = 40
PARTS = 4
LAME = 0.3 / (1.3 * 0.4)
SHEAR = 1.0 / 2.6

DIRECTIONS = sorted((d for d in itertools.product((-1, 0, 1), repeat=3) if any(d)), key=lambda d: (not d[1], sum(map(abs, d))))
LOWER = [d for d in DIRECTIONS if max(d) <= 0]


def slot(direction):
    return (direction[0] + 1) * 9 + (direction[1] + 1) * 3 + direction[2] + 1


def lower_slot(direction):
    return -(direction[0] * 4 + direction[1] * 2 + direction[2])


def iota(shape, axis):
    return lax.broadcasted_iota(jnp.int32, shape, axis)


def hat_lanes(v):
    lane = iota(v.shape, v.ndim - 1)
    axis = v.ndim - 1

    def moved(step):
        rolled = pltpu.roll(v, step % NZ, axis)
        return jnp.where(lane >= step if step > 0 else lane < NZ + step, rolled, 0.0)

    return 3.0 * v + 2.0 * (moved(1) + moved(-1)) + (moved(2) + moved(-2))


def across(v, axis, size, step, direction):
    place = iota(v.shape, axis) // step
    count = size // step
    if direction > 0:
        two, one = pltpu.roll(v, 2 * step, axis), pltpu.roll(v, step, axis)
        return jnp.where(place == 0, two + 2.0 * one, jnp.where(place == 1, two, 0.0))
    two, one = pltpu.roll(v, size - 2 * step, axis), pltpu.roll(v, size - step, axis)
    return jnp.where(place == count - 1, two + 2.0 * one, jnp.where(place == count - 2, two, 0.0))


def rows_at(places):
    row = iota((8, NZ), 0)
    tile = jnp.zeros((8, NZ), F32)
    for place, value in places.items():
        tile = jnp.where(row == place, jnp.broadcast_to(value, (8, NZ)), tile)
    return tile


def kernel(sizes, density, displacement, out, total_out, *scratch):
    (field, g, b4, acc, rows, corner, nodes, sd, energy,
     xs, ys, xys, zs, xzs, yzs, xyzs, xr, yr, xyr, zr, xzr, yzr, xyzr,
     dys, dxys, dzs, dxzs, dyzs, dxyzs, dxyr, dzr, dxzr, dyzr, dxyzr, m6,
     part, part_in, send_sem, recv_sem, dsend_sem, drecv_sem, load_sem, psend_sem, precv_sem) = scratch
    size_x, size_y, size_z, ring_y = sizes
    gx, gy, gz = (lax.axis_index(a) for a in ("gx", "gy", "gz"))

    def inside(direction):
        ok = []
        for place, step, count in zip((gx, gy, gz), direction, (size_x, size_y, size_z)):
            if step > 0:
                ok.append(place < count - 1)
            elif step < 0:
                ok.append(place > 0)
        return functools.reduce(jnp.logical_and, ok)

    def device(direction):
        return (gx + direction[0], gy + direction[1], gz + direction[2])

    layers_z = size_x // ring_y
    my_y, my_z = lax.rem(gx, ring_y), gx // ring_y + layers_z * (gy // 2)
    my_core = lax.rem(gy, 2)
    count_z = layers_z * (size_y // 2)

    halves = size_y // 2
    early = gy < 2

    def at_zc(z, c):
        return (lax.rem(z, layers_z) * ring_y + my_y, (z // layers_z) * 2 + c, gz)

    def partner_xy(dx, dy):
        x, y = lax.rem(gz + dx, size_z), lax.rem(my_y + dy, ring_y)
        return ((gx // ring_y) * ring_y + y, gy, x)

    mirror = at_zc(count_z - 1 - my_z, my_core)
    column = [(z, c) for z in range(layers_z) for c in range(2)]

    def other(z, c):
        return jnp.logical_or(my_z != z, my_core != c)

    def far_first(counts):
        offs = [o for o in itertools.product(*[range(c) for c in counts]) if any(o)]
        return sorted(offs, key=lambda o: -sum(min(s, c - s) for s, c in zip(o, counts)))

    plane = far_first((size_z, ring_y))

    load_density = pltpu.make_async_copy(density, field.at[pl.ds(2 * NY, ROWS)], load_sem.at[0])
    load_nodes = pltpu.make_async_copy(displacement, nodes.at[:, pl.ds(0, ROWS)], load_sem.at[1])
    load_density.start()
    load_nodes.start()

    barrier = pltpu.get_barrier_semaphore()

    def greet(to):
        pl.semaphore_signal(barrier, inc=1, device_id=to, device_id_type=MESH)

    waits = 0
    for d in DIRECTIONS:
        @pl.when(inside(d))
        def _(d=d):
            greet(device(d))
        waits = waits + inside(d).astype(jnp.int32)

    @pl.when(early)
    def _():
        for z, c in [(z, c) for z in range(count_z) for c in range(2)]:
            @pl.when(other(z, c))
            def _(z=z, c=c):
                greet(at_zc(z, c))
        for o in plane:
            greet(partner_xy(*o))

    if halves > 1:
        @pl.when(jnp.logical_not(early))
        def _():
            greet(mirror)

    waits = waits + jnp.where(early, 2 * layers_z - 1 + len(plane) + (halves - 1), 2 * layers_z)

    zero_row = jnp.zeros((8, NZ), F32)

    def zero(ref):
        ref[...] = jnp.zeros(ref.shape, F32)

    received = {}
    for d in DIRECTIONS:
        sx, sy, sz = ((s + 1) // 2 for s in d)
        kind = tuple(bool(s) for s in d)
        received[d] = {
            (True, False, False): lambda p: (xs.at[p, sx], xr.at[p, sx]),
            (False, True, False): lambda p: (ys.at[p, sy], yr.at[p, sy]),
            (True, True, False): lambda p: (xys.at[p, sx, sy], xyr.at[p, sx, sy]),
            (False, False, True): lambda p: (zs.at[p, sz], zr.at[p, sz]),
            (True, False, True): lambda p: (xzs.at[p, sx, sz], xzr.at[p, sx, sz]),
            (False, True, True): lambda p: (yzs.at[p, sy, sz], yzr.at[p, sy, sz]),
            (True, True, True): lambda p: (xyzs.at[p, sx, sy, sz], xyzr.at[p, sx, sy, sz]),
        }[kind]
        received[d] = [received[d](p) for p in range(2)]
    lower = {
        (-1, 0, 0): (nodes.at[:, pl.ds(0, NY)], nodes.at[:, pl.ds(ROWS, NY)]),
        (0, -1, 0): (dys, nodes.at[:, pl.ds(ROWS + NY, NX)]),
        (-1, -1, 0): (dxys, dxyr),
        (0, 0, -1): (dzs, dzr),
        (-1, 0, -1): (dxzs, dxzr),
        (0, -1, -1): (dyzs, dyzr),
        (-1, -1, -1): (dxyzs, dxyzr),
    }

    for d in DIRECTIONS:
        @pl.when(jnp.logical_not(inside(tuple(-s for s in d))))
        def _(d=d):
            for p in range(2):
                zero(received[d][p][1])
            if d in lower:
                zero(lower[d][1])

    def remote(source, target, send, recv, to):
        return pltpu.make_async_remote_copy(
            src_ref=source, dst_ref=target, send_sem=send, recv_sem=recv, device_id=to, device_id_type=MESH)

    def filter_copy(p, d):
        source, target = received[d][p]
        return remote(source, target, send_sem.at[p, slot(d)], recv_sem.at[p, slot(d)], device(d))

    def lower_copy(d):
        source, target = lower[d]
        return remote(source, target, dsend_sem.at[lower_slot(d)], drecv_sem.at[lower_slot(d)], device(d))

    for margin in (0, NY, (NX + 2) * NY, (NX + 3) * NY):
        field[pl.ds(margin, NY), :] = jnp.zeros((NY, NZ), F32)

    for i in range(NX):
        g[pl.ds(i * YPAD, 8), :] = zero_row
        g[pl.ds(i * YPAD + 40, 8), :] = zero_row
    for i in range(4):
        b4[pl.ds(i * YPAD, 8), :] = zero_row
        b4[pl.ds(i * YPAD + 40, 8), :] = zero_row
    zero(rows)
    zero(corner)
    zero(m6)

    middle = jnp.zeros((112, 128), F32)

    def hat_rows(ref, base):
        at = [ref[pl.ds(base + 6 + k, NY), :] for k in range(5)]
        return 3.0 * at[2] + 2.0 * (at[1] + at[3]) + (at[0] + at[4])

    def store_pair(ref, tile, first):
        ref[0] = tile[first:first + 1]
        ref[1] = tile[first + 1:first + 2]

    def z_edges(low, high):
        return jnp.concatenate([
            rows_at({0: low[0] + 2.0 * low[1], 1: low[1]}), middle,
            rows_at({6: high[0], 7: 2.0 * high[0] + high[1]})], 0).T

    def local_filter(p, ref):
        for n, layer in enumerate((0, 1, NX - 2, NX - 1)):
            b4[pl.ds(n * YPAD + 8, NY), :] = field[pl.ds((layer + 2) * NY, NY), :]
        faces = [hat_rows(b4, n * YPAD) for n in range(4)]
        for n in range(4):
            xs[p, n // 2, pl.ds((n % 2) * NY, NY), :] = hat_lanes(faces[n])
        turned = jnp.concatenate(faces, 0).T
        for sz, part_z in enumerate((turned[0:8], turned[120:128])):
            for sx in range(2):
                store_pair(xzs.at[p, sx, sz], across(part_z, 1, 128, 32, 2 * sx - 1), 6 * sz)

        for t in range(NY // 8):
            at = [field[pl.ds(i * NY + 8 * t, 8), :] for i in range(NX + 4)]
            for i in range(NX):
                g[pl.ds(i * YPAD + 8 + 8 * t, 8), :] = (
                    3.0 * at[i + 2] + 2.0 * (at[i + 1] + at[i + 3]) + (at[i] + at[i + 4]))

        for n, row in enumerate((0, 1, NY - 2, NY - 1)):
            edge = g[pl.ds(8 + row, NX, stride=YPAD), :]
            rows[pl.ds(n * 32, NX), :] = edge
            ys[p, n // 2, n % 2] = hat_lanes(edge)
            raw = field[pl.ds(2 * NY + row, NX, stride=NY), :]
            up, down = across(raw[NX - 8:], 0, 8, 1, 1), across(raw[:8], 0, 8, 1, -1)
            corner[pl.ds(n * 32, 8), :] = up
            corner[pl.ds(n * 32 + NX - 8, 8), :] = down
            store_pair(xys.at[p, 1, n // 2, pl.ds(2 * (n % 2), 2)], hat_lanes(up), 0)
            store_pair(xys.at[p, 0, n // 2, pl.ds(2 * (n % 2), 2)], hat_lanes(down), 6)
        turned = rows[...].T
        for sz, part_z in enumerate((turned[0:8], turned[120:128])):
            for sy in range(2):
                store_pair(yzs.at[p, sy, sz], across(part_z, 1, 128, 32, 2 * sy - 1), 6 * sz)
        turned = corner[...].T
        lane = lax.rem(iota((8, 128), 1), 32)
        for sz, part_z in enumerate((turned[0:8], turned[120:128])):
            for sy in range(2):
                both = across(part_z, 1, 128, 32, 2 * sy - 1)
                store_pair(xyzs.at[p, 1, sy, sz], jnp.where(lane < 8, both, 0.0), 6 * sz)
                store_pair(xyzs.at[p, 0, sy, sz], jnp.where(lane < 8, 0.0, both), 6 * sz)

        for k in range(GROUPS):
            v = jnp.concatenate([hat_rows(g, (4 * k + n) * YPAD) for n in range(4)], 0)
            ref[pl.ds(k * 128, 128), :] = hat_lanes(v)
            turned = v.T
            store_pair(zs.at[p, 0, pl.ds(2 * k, 2)], turned[0:8], 0)
            store_pair(zs.at[p, 1, pl.ds(2 * k, 2)], turned[120:128], 6)

    def send_filter(p):
        for d in DIRECTIONS:
            @pl.when(inside(d))
            def _(d=d):
                filter_copy(p, d).start()

    def wait_received(p, along_y):
        for d in DIRECTIONS:
            if bool(d[1]) == along_y:
                @pl.when(inside(tuple(-s for s in d)))
                def _(d=d):
                    filter_copy(p, d).wait_recv()

    def add_xz(p, acc):
        wait_received(p, False)
        def add(layer, v):
            acc[pl.ds(layer * NY, NY), :] = acc[pl.ds(layer * NY, NY), :] + v

        first, second = xr[p, 1, pl.ds(0, NY), :], xr[p, 1, pl.ds(NY, NY), :]
        add(0, first + 2.0 * second)
        add(1, second)
        first, second = xr[p, 0, pl.ds(0, NY), :], xr[p, 0, pl.ds(NY, NY), :]
        add(NX - 2, first)
        add(NX - 1, 2.0 * first + second)
        for k in range(GROUPS):
            low, high = [[zr[p, sz, 2 * k + i] for i in range(2)] for sz in (1, 0)]
            edge = {0: 1, GROUPS - 1: 0}.get(k)
            if edge is not None:
                low, high = [[v[i] + xzr[p, edge, sz, i] for i in range(2)] for v, sz in ((low, 1), (high, 0))]
            acc[pl.ds(k * 128, 128), :] = acc[pl.ds(k * 128, 128), :] + z_edges(low, high)

    def add_y(p, acc):
        wait_received(p, True)
        low, high = [[sum([yzr[p, sy, sz, i] for sy in range(2)] + [
            xyzr[p, sx, sy, sz, i] for sx in range(2) for sy in range(2)]) for i in range(2)] for sz in (1, 0)]
        turned = z_edges(low, high)
        at = {}
        for sy in range(2):
            for n in range(2):
                center = yr[p, sy, n]
                up, down = [[xyr[p, sx, sy, 2 * n + i] for i in range(2)] for sx in (1, 0)]
                at[sy, n] = jnp.concatenate([
                    center[:8] + rows_at({0: up[0], 1: up[1]}), center[8:16],
                    center[16:] + rows_at({6: down[0], 7: down[1]})], 0)
        for n, (row, v) in enumerate((
                (0, at[1, 0] + 2.0 * at[1, 1]), (1, at[1, 1]), (NY - 2, at[0, 0]), (NY - 1, 2.0 * at[0, 0] + at[0, 1]))):
            place = pl.ds(row, NX, stride=NY)
            acc[place, :] = acc[place, :] + v + turned[n * 32:n * 32 + NX]

    load_density.wait()
    local_filter(0, acc)
    load_nodes.wait()

    def first_columns(v):
        lane = iota(v[0].shape, 1)
        return jnp.where(lane == 0, v[0], jnp.where(
            lane == 1, pltpu.roll(v[1], 1, 1), jnp.where(lane == 2, pltpu.roll(v[2], 2, 1), 0.0)))

    for m in range(3):
        dys[m] = nodes[m, pl.ds(0, NX, stride=NY), :]
        dxys[m] = dys[m, pl.ds(0, 1), :]
    for k in range(GROUPS):
        columns = first_columns([nodes[m, pl.ds(k * 128, 128), :] for m in range(3)])
        turned = columns.T[0:8]
        for m in range(3):
            dzs[3 * k + m] = turned[m:m + 1]
        if k == 0:
            m6[pl.ds(0, NY), :] = columns[:NY]
    m6[pl.ds(NY, NX), :] = first_columns([dys[m] for m in range(3)])
    turned = m6[...].T[0:8]
    lane8 = iota((8, 128), 1)
    for target, tile in (
            (dxzs, jnp.where(lane8 < NY, turned, 0.0)),
            (dyzs, jnp.where(jnp.logical_and(lane8 >= NY, lane8 < NY + NX), turned, 0.0)),
            (dxyzs, jnp.where(lane8 == NY + NX, pltpu.roll(turned, NY + NX, 1), 0.0))):
        for m in range(3):
            target[m] = tile[m:m + 1]

    pl.semaphore_wait(barrier, waits)
    for d in LOWER:
        @pl.when(inside(d))
        def _(d=d):
            lower_copy(d).start()
    send_filter(0)

    def wait_lower(along_y):
        for d in LOWER:
            if bool(d[1]) == along_y:
                @pl.when(inside(tuple(-s for s in d)))
                def _(d=d):
                    lower_copy(d).wait_recv()

    rest = jnp.zeros((120, 128), F32)

    def z_pass(base, count, packed):
        halo = jnp.concatenate([rows_at(dict(enumerate(packed))), rest], 0).T[:count]
        lane = iota(halo.shape, 1)
        out = []
        for m in range(3):
            u = nodes[m, pl.ds(base, count), :]
            up = jnp.where(lane == NZ - 1, pltpu.roll(halo, NZ - 1 - m, 1), pltpu.roll(u, NZ - 1, 1))
            out += [u + up, up - u]
        return out

    wait_lower(False)
    for k in range(GROUPS):
        for n, v in enumerate(z_pass(k * 128, 128, [dzr[3 * k + m] for m in range(3)])):
            for i in range(4):
                sd[n, pl.ds((4 * k + i) * NODE_PAD, NY), :] = v[i * NY:(i + 1) * NY]
    for n, v in enumerate(z_pass(ROWS, NY, [dxzr[m] for m in range(3)])):
        sd[n, pl.ds(NX * NODE_PAD, NY), :] = v

    def yz_terms(i, t):
        base = pl.multiple_of(i * NODE_PAD, 8) + 8 * t
        out = []
        for k in range(6):
            here, above = sd[k, pl.ds(base, 8), :], sd[k, pl.ds(base + 1, 8), :]
            out += [here + above, above - here]
        return out

    square = lambda v: v * v

    def energies(t):
        def element(i, before):
            now = yz_terms(i, t)
            w = []
            for m in range(3):
                (a0, a1, a2, a3), (b0, b1, b2, b3) = now[4 * m:4 * m + 4], before[4 * m:4 * m + 4]
                w.append({100: a0 - b0, 110: a1 - b1, 101: a2 - b2, 111: a3 - b3,
                          10: a1 + b1, 1: a2 + b2, 11: a3 + b3})
            u, v, z = w
            total = (LAME / 16) * square(u[100] + v[10] + z[1])
            total += (LAME / 48) * (square(v[110] + z[101]) + square(u[110] + z[11]) + square(u[101] + v[11]))
            total += (SHEAR / 8) * (square(u[100]) + square(v[10]) + square(z[1]))
            total += (SHEAR / 16) * (
                (square(u[110]) + square(u[101]) + square(v[110])) + (square(v[11]) + square(z[101]) + square(z[11]))
                + (square(u[10] + v[100]) + square(v[1] + z[10]) + square(u[1] + z[100])))
            total += (SHEAR / 48) * (square(u[11] + v[101]) + square(v[101] + z[110]) + square(u[11] + z[110]))
            total += ((LAME + 4 * SHEAR) / 144) * (square(u[111]) + square(v[111]) + square(z[111]))
            energy[pl.ds(pl.multiple_of((i - 1) * NY, NY) + 8 * t, 8), :] = total
            return now

        def pair(n, before):
            return tuple(element(2 * n + 2, element(2 * n + 1, before)))

        lax.fori_loop(0, NX // 2, pair, tuple(yz_terms(0, t)))

    for t in range(NY // 8 - 1):
        energies(t)
    add_xz(0, acc)
    wait_lower(True)
    for m in range(3):
        nodes[m, pl.ds(ROWS + NY + NX, 1), :] = dxyr[m]
    for n, v in enumerate(z_pass(ROWS + NY, NY, [pltpu.roll(dyzr[m] + dxyzr[m], 128 - NY, 1) for m in range(3)])):
        sd[n, pl.ds(NY, NX + 1, stride=NODE_PAD), :] = v[:NX + 1]
    energies(NY // 8 - 1)

    add_y(0, acc)

    def inverse_cover(index, extent):
        end = extent - 1
        return jnp.where(jnp.logical_or(index == 0, index == end), 1.0 / 6.0, jnp.where(
            jnp.logical_or(index == 1, index == end - 1), 1.0 / 8.0, 1.0 / 9.0)).astype(F32)

    inverse_yz = inverse_cover(iota((NY, NZ), 0) + gy * NY, NY * size_y) * inverse_cover(
        iota((NY, NZ), 1) + gz * NZ, NZ * size_z)

    total = jnp.zeros((NY, NZ), F32)
    for i in range(NX):
        inverse = inverse_yz * inverse_cover(gx * NX + i, NX * size_x)
        physical = acc[pl.ds(i * NY, NY), :] * inverse
        product = physical * physical * energy[pl.ds(i * NY, NY), :]
        field[pl.ds((i + 2) * NY, NY), :] = -3.0 * product * inverse
        total = total + physical * product
    total = jnp.sum(total, axis=0, keepdims=True)

    def sum_copy(s, mine, to):
        return remote(part.at[s], part_in.at[s, mine], psend_sem.at[s], precv_sem.at[s], to)

    def sum_wait(sem, s, n):
        whole = part_in.at[s, pl.ds(0, n)]
        pltpu.make_async_copy(whole, whole, sem.at[s]).wait()

    mine = my_z * 2 + my_core
    part[0] = total
    for z, c in column:
        @pl.when(other(z, c))
        def _(z=z, c=c):
            sum_copy(0, mine, at_zc(z, c)).start()
    local_filter(1, out)
    send_filter(1)

    @pl.when(early)
    def _():
        part_in[0, mine] = total
        sum_wait(precv_sem, 0, 2 * count_z - 1)
        partial = jnp.sum(part_in[0, 0:2 * count_z], axis=0)
        here = gz * ring_y + my_y
        part[1] = partial
        part_in[1, here] = partial
        for o in plane:
            sum_copy(1, here, partner_xy(*o)).start()

    add_xz(1, out)
    add_y(1, out)

    @pl.when(early)
    def _():
        sum_wait(precv_sem, 1, len(plane))
        final = jnp.sum(part_in[1, 0:len(plane) + 1], axis=0)
        part[2] = final
        if halves > 1:
            sum_copy(2, 0, mirror).start()
            sum_copy(2, 0, mirror).wait_send()
        sum_wait(psend_sem, 1, len(plane))
        sum_wait(psend_sem, 0, 2 * layers_z - 1)

    @pl.when(jnp.logical_not(early))
    def _():
        if halves > 1:
            sum_wait(precv_sem, 2, 1)
            part[2] = part_in[2, 0]
        sum_wait(psend_sem, 0, 2 * layers_z)

    total_out[...] = jnp.broadcast_to(jnp.sum(part[2], axis=1, keepdims=True), (8, 128))

    for d in DIRECTIONS:
        @pl.when(inside(d))
        def _(d=d):
            for p in range(2):
                filter_copy(p, d).wait_send()
            if d in lower:
                lower_copy(d).wait_send()


def exchange(mesh, density, displacement):
    sizes = (mesh.shape["gx"], mesh.shape["gy"], mesh.shape["gz"], min(8, mesh.shape["gx"]))
    vmem = lambda *shape: pltpu.VMEM(shape, F32)
    partners = max(sizes[0] // sizes[3] * sizes[1], sizes[3] * sizes[2])
    scratch = [
        vmem((NX + 4) * NY, NZ), vmem(NX * YPAD, NZ), vmem(4 * YPAD, NZ), vmem(ROWS, NZ),
        vmem(128, NZ), vmem(128, NZ), vmem(3, ROWS + 2 * NY, NZ),
        vmem(6, (NX + 1) * NODE_PAD, NZ), vmem(ROWS, NZ)]
    filters = [vmem(2, 2, 2 * NY, NZ), vmem(2, 2, 2, NX, NZ), vmem(2, 2, 2, 4, 1, NZ), vmem(2, 2, 2 * GROUPS, 1, 128),
               vmem(2, 2, 2, 2, 1, 128), vmem(2, 2, 2, 2, 1, 128), vmem(2, 2, 2, 2, 2, 1, 128)]
    scratch += filters + filters
    edges = [vmem(3, 1, NZ), vmem(3 * GROUPS, 1, 128), vmem(3, 1, 128), vmem(3, 1, 128), vmem(3, 1, 128)]
    scratch += [vmem(3, NX, NZ)] + edges + edges + [vmem(128, 128)]
    scratch += [vmem(3, 1, 128), vmem(3, partners, 1, 128)]
    dma = pltpu.SemaphoreType.DMA
    scratch += [dma((2, 27)), dma((2, 27)), dma((8,)), dma((8,)), dma((2,)), dma((3,)), dma((3,))]
    return pl.pallas_call(
        functools.partial(kernel, sizes),
        out_shape=[jax.ShapeDtypeStruct((ROWS, NZ), F32), jax.ShapeDtypeStruct((8, 128), F32)],
        in_specs=[pl.BlockSpec(memory_space=pltpu.HBM)] * 2,
        out_specs=[pl.BlockSpec(memory_space=pltpu.VMEM)] * 2,
        scratch_shapes=scratch,
        compiler_params=pltpu.CompilerParams(
            collective_id=0, has_side_effects=True, vmem_limit_bytes=56_000_000),
        cost_estimate=pl.CostEstimate(flops=20_000_000, bytes_accessed=2_000_000, transcendentals=0),
    )(density, displacement)


def scale_kernel(elements, field, total, out, mean_out, scaled, sem):
    mean = total[0:1, :] / elements
    mean_out[...] = mean[:, 0:1]
    inverse = 1.0 / mean
    copies = []
    for n in range(PARTS):
        part = pl.ds(n * (ROWS // PARTS), ROWS // PARTS)
        scaled[part, :] = field[part, :] * inverse
        copies.append(pltpu.make_async_copy(scaled.at[part], out.at[part], sem.at[n]))
        copies[-1].start()
    for copy in copies:
        copy.wait()


def solution(mesh):
    def shards(displacement, density):
        filtered, total = exchange(mesh, density.reshape(ROWS, NZ), displacement.reshape(3, ROWS, NZ))
        sensitivity, mean = pl.pallas_call(
            functools.partial(scale_kernel, float(ROWS * NZ * mesh.size)),
            out_shape=[jax.ShapeDtypeStruct((ROWS, NZ), F32), jax.ShapeDtypeStruct((1, 1), F32)],
            in_specs=[pl.BlockSpec(memory_space=pltpu.VMEM)] * 2,
            out_specs=[pl.BlockSpec(memory_space=pl.ANY), pl.BlockSpec((1, 1), lambda: (0, 0))],
            scratch_shapes=[pltpu.VMEM((ROWS, NZ), F32), pltpu.SemaphoreType.DMA((PARTS,))],
            compiler_params=pltpu.CompilerParams(vmem_limit_bytes=4 * 2**20),
        )(filtered, total)
        return sensitivity.reshape(NX, NY, NZ), mean.reshape(())

    return jax.shard_map(
        shards,
        mesh=mesh,
        in_specs=(P(None, "gx", "gy", "gz"), P("gx", "gy", "gz")),
        out_specs=(P("gx", "gy", "gz"), P()),
        check_vma=False,
    )
```

```python
import functools
import itertools

import jax
import jax.numpy as jnp
from jax import lax
from jax.experimental import pallas as pl
from jax.experimental.pallas import tpu as pltpu
from jax.sharding import PartitionSpec as P

MESH = pl.DeviceIdType.MESH
F32 = jnp.float32
NX, NY, NZ = 24, 32, 128
ROWS = NX * NY
GROUPS = ROWS // 128
YPAD = 48
NODE_PAD = 40
PARTS = 4
LAME = 0.3 / (1.3 * 0.4)
SHEAR = 1.0 / 2.6

DIRECTIONS = sorted((d for d in itertools.product((-1, 0, 1), repeat=3) if any(d)), key=lambda d: (not d[1], sum(map(abs, d))))
LOWER = [d for d in DIRECTIONS if max(d) <= 0]


def slot(direction):
    return (direction[0] + 1) * 9 + (direction[1] + 1) * 3 + direction[2] + 1


def lower_slot(direction):
    return -(direction[0] * 4 + direction[1] * 2 + direction[2])


def iota(shape, axis):
    return lax.broadcasted_iota(jnp.int32, shape, axis)


def hat_lanes(v):
    lane = iota(v.shape, v.ndim - 1)
    axis = v.ndim - 1

    def moved(step):
        rolled = pltpu.roll(v, step % NZ, axis)
        return jnp.where(lane >= step if step > 0 else lane < NZ + step, rolled, 0.0)

    return 3.0 * v + 2.0 * (moved(1) + moved(-1)) + (moved(2) + moved(-2))


def across(v, axis, size, step, direction):
    place = iota(v.shape, axis) // step
    count = size // step
    if direction > 0:
        two, one = pltpu.roll(v, 2 * step, axis), pltpu.roll(v, step, axis)
        return jnp.where(place == 0, two + 2.0 * one, jnp.where(place == 1, two, 0.0))
    two, one = pltpu.roll(v, size - 2 * step, axis), pltpu.roll(v, size - step, axis)
    return jnp.where(place == count - 1, two + 2.0 * one, jnp.where(place == count - 2, two, 0.0))


def rows_at(places):
    row = iota((8, NZ), 0)
    tile = jnp.zeros((8, NZ), F32)
    for place, value in places.items():
        tile = jnp.where(row == place, jnp.broadcast_to(value, (8, NZ)), tile)
    return tile


def kernel(sizes, density, displacement, out, total_out, *scratch):
    (field, g, b4, acc, rows, corner, nodes, sd, energy,
     xs, ys, xys, zs, xzs, yzs, xyzs, xr, yr, xyr, zr, xzr, yzr, xyzr,
     dys, dxys, dzs, dxzs, dyzs, dxyzs, dxyr, dzr, dxzr, dyzr, dxyzr, m6,
     part, part_in, send_sem, recv_sem, dsend_sem, drecv_sem, load_sem, psend_sem, precv_sem, pass_sem) = scratch
    size_x, size_y, size_z, ring_y = sizes
    gx, gy, gz = (lax.axis_index(a) for a in ("gx", "gy", "gz"))

    def inside(direction):
        ok = []
        for place, step, count in zip((gx, gy, gz), direction, (size_x, size_y, size_z)):
            if step > 0:
                ok.append(place < count - 1)
            elif step < 0:
                ok.append(place > 0)
        return functools.reduce(jnp.logical_and, ok)

    def device(direction):
        return (gx + direction[0], gy + direction[1], gz + direction[2])

    layers_z = size_x // ring_y
    my_y, my_z = lax.rem(gx, ring_y), gx // ring_y + layers_z * (gy // 2)
    my_core = lax.rem(gy, 2)
    count_z = layers_z * (size_y // 2)

    halves = size_y // 2
    early = gy < 2

    def at_zc(z, c):
        return (lax.rem(z, layers_z) * ring_y + my_y, (z // layers_z) * 2 + c, gz)

    def partner_xy(dx, dy):
        x, y = lax.rem(gz + dx, size_z), lax.rem(my_y + dy, ring_y)
        return ((gx // ring_y) * ring_y + y, gy, x)

    server = layers_z - 1 - (my_z - layers_z) // 2
    serves = [z for z in range(layers_z, count_z)]

    def served_from(z):
        return layers_z - 1 - (z - layers_z) // 2

    column = [(z, c) for z in range(layers_z) for c in range(2)]

    def other(z, c):
        return jnp.logical_or(my_z != z, my_core != c)

    def far_first(counts):
        offs = [o for o in itertools.product(*[range(c) for c in counts]) if any(o)]
        return sorted(offs, key=lambda o: -sum(min(s, c - s) for s, c in zip(o, counts)))

    plane = far_first((size_z, ring_y))

    load_density = pltpu.make_async_copy(density, field.at[pl.ds(2 * NY, ROWS)], load_sem.at[0])
    load_nodes = pltpu.make_async_copy(displacement, nodes.at[:, pl.ds(0, ROWS)], load_sem.at[1])
    load_density.start()
    load_nodes.start()

    barrier = pltpu.get_barrier_semaphore()

    def greet(to):
        pl.semaphore_signal(barrier, inc=1, device_id=to, device_id_type=MESH)

    waits = 0
    for d in DIRECTIONS:
        @pl.when(inside(d))
        def _(d=d):
            greet(device(d))
        waits = waits + inside(d).astype(jnp.int32)

    @pl.when(early)
    def _():
        for z, c in [(z, c) for z in range(count_z) for c in range(2)]:
            @pl.when(other(z, c))
            def _(z=z, c=c):
                greet(at_zc(z, c))
        for o in plane:
            greet(partner_xy(*o))

    if halves > 1:
        @pl.when(jnp.logical_not(early))
        def _():
            greet(at_zc(server, my_core))

    served = sum((my_z == served_from(z)).astype(jnp.int32) for z in serves) if serves else 0
    waits = waits + jnp.where(early, 2 * layers_z - 1 + len(plane) + served, 2 * layers_z)

    zero_row = jnp.zeros((8, NZ), F32)

    def zero(ref):
        ref[...] = jnp.zeros(ref.shape, F32)

    received = {}
    for d in DIRECTIONS:
        sx, sy, sz = ((s + 1) // 2 for s in d)
        kind = tuple(bool(s) for s in d)
        received[d] = {
            (True, False, False): lambda p: (xs.at[p, sx], xr.at[p, sx]),
            (False, True, False): lambda p: (ys.at[p, sy], yr.at[p, sy]),
            (True, True, False): lambda p: (xys.at[p, sx, sy], xyr.at[p, sx, sy]),
            (False, False, True): lambda p: (zs.at[p, sz], zr.at[p, sz]),
            (True, False, True): lambda p: (xzs.at[p, sx, sz], xzr.at[p, sx, sz]),
            (False, True, True): lambda p: (yzs.at[p, sy, sz], yzr.at[p, sy, sz]),
            (True, True, True): lambda p: (xyzs.at[p, sx, sy, sz], xyzr.at[p, sx, sy, sz]),
        }[kind]
        received[d] = [received[d](p) for p in range(2)]
    lower = {
        (-1, 0, 0): (nodes.at[:, pl.ds(0, NY)], nodes.at[:, pl.ds(ROWS, NY)]),
        (0, -1, 0): (dys, nodes.at[:, pl.ds(ROWS + NY, NX)]),
        (-1, -1, 0): (dxys, dxyr),
        (0, 0, -1): (dzs, dzr),
        (-1, 0, -1): (dxzs, dxzr),
        (0, -1, -1): (dyzs, dyzr),
        (-1, -1, -1): (dxyzs, dxyzr),
    }

    for d in DIRECTIONS:
        @pl.when(jnp.logical_not(inside(tuple(-s for s in d))))
        def _(d=d):
            for p in range(2):
                zero(received[d][p][1])
            if d in lower:
                zero(lower[d][1])

    def remote(source, target, send, recv, to):
        return pltpu.make_async_remote_copy(
            src_ref=source, dst_ref=target, send_sem=send, recv_sem=recv, device_id=to, device_id_type=MESH)

    def filter_copy(p, d):
        source, target = received[d][p]
        return remote(source, target, send_sem.at[p, slot(d)], recv_sem.at[p, slot(d)], device(d))

    def lower_copy(d):
        source, target = lower[d]
        return remote(source, target, dsend_sem.at[lower_slot(d)], drecv_sem.at[lower_slot(d)], device(d))

    for margin in (0, NY, (NX + 2) * NY, (NX + 3) * NY):
        field[pl.ds(margin, NY), :] = jnp.zeros((NY, NZ), F32)

    for i in range(NX):
        g[pl.ds(i * YPAD, 8), :] = zero_row
        g[pl.ds(i * YPAD + 40, 8), :] = zero_row
    for i in range(4):
        b4[pl.ds(i * YPAD, 8), :] = zero_row
        b4[pl.ds(i * YPAD + 40, 8), :] = zero_row
    zero(rows)
    zero(corner)
    zero(m6)

    middle = jnp.zeros((112, 128), F32)

    def hat_rows(ref, base):
        at = [ref[pl.ds(base + 6 + k, NY), :] for k in range(5)]
        return 3.0 * at[2] + 2.0 * (at[1] + at[3]) + (at[0] + at[4])

    def store_pair(ref, tile, first):
        ref[0] = tile[first:first + 1]
        ref[1] = tile[first + 1:first + 2]

    def z_edges(low, high):
        return jnp.concatenate([
            rows_at({0: low[0] + 2.0 * low[1], 1: low[1]}), middle,
            rows_at({6: high[0], 7: 2.0 * high[0] + high[1]})], 0).T

    def local_filter(p, ref):
        for n, layer in enumerate((0, 1, NX - 2, NX - 1)):
            b4[pl.ds(n * YPAD + 8, NY), :] = field[pl.ds((layer + 2) * NY, NY), :]
        faces = [hat_rows(b4, n * YPAD) for n in range(4)]
        for n in range(4):
            xs[p, n // 2, pl.ds((n % 2) * NY, NY), :] = hat_lanes(faces[n])
        turned = jnp.concatenate(faces, 0).T
        for sz, part_z in enumerate((turned[0:8], turned[120:128])):
            for sx in range(2):
                store_pair(xzs.at[p, sx, sz], across(part_z, 1, 128, 32, 2 * sx - 1), 6 * sz)

        for t in range(NY // 8):
            at = [field[pl.ds(i * NY + 8 * t, 8), :] for i in range(NX + 4)]
            for i in range(NX):
                g[pl.ds(i * YPAD + 8 + 8 * t, 8), :] = (
                    3.0 * at[i + 2] + 2.0 * (at[i + 1] + at[i + 3]) + (at[i] + at[i + 4]))

        for n, row in enumerate((0, 1, NY - 2, NY - 1)):
            edge = g[pl.ds(8 + row, NX, stride=YPAD), :]
            rows[pl.ds(n * 32, NX), :] = edge
            ys[p, n // 2, n % 2] = hat_lanes(edge)
            raw = field[pl.ds(2 * NY + row, NX, stride=NY), :]
            up, down = across(raw[NX - 8:], 0, 8, 1, 1), across(raw[:8], 0, 8, 1, -1)
            corner[pl.ds(n * 32, 8), :] = up
            corner[pl.ds(n * 32 + NX - 8, 8), :] = down
            store_pair(xys.at[p, 1, n // 2, pl.ds(2 * (n % 2), 2)], hat_lanes(up), 0)
            store_pair(xys.at[p, 0, n // 2, pl.ds(2 * (n % 2), 2)], hat_lanes(down), 6)
        turned = rows[...].T
        for sz, part_z in enumerate((turned[0:8], turned[120:128])):
            for sy in range(2):
                store_pair(yzs.at[p, sy, sz], across(part_z, 1, 128, 32, 2 * sy - 1), 6 * sz)
        turned = corner[...].T
        lane = lax.rem(iota((8, 128), 1), 32)
        for sz, part_z in enumerate((turned[0:8], turned[120:128])):
            for sy in range(2):
                both = across(part_z, 1, 128, 32, 2 * sy - 1)
                store_pair(xyzs.at[p, 1, sy, sz], jnp.where(lane < 8, both, 0.0), 6 * sz)
                store_pair(xyzs.at[p, 0, sy, sz], jnp.where(lane < 8, 0.0, both), 6 * sz)

        for k in range(GROUPS):
            v = jnp.concatenate([hat_rows(g, (4 * k + n) * YPAD) for n in range(4)], 0)
            ref[pl.ds(k * 128, 128), :] = hat_lanes(v)
            turned = v.T
            store_pair(zs.at[p, 0, pl.ds(2 * k, 2)], turned[0:8], 0)
            store_pair(zs.at[p, 1, pl.ds(2 * k, 2)], turned[120:128], 6)

    def send_filter(p):
        for d in DIRECTIONS:
            @pl.when(inside(d))
            def _(d=d):
                filter_copy(p, d).start()

    def wait_received(p, along_y):
        for d in DIRECTIONS:
            if bool(d[1]) == along_y:
                @pl.when(inside(tuple(-s for s in d)))
                def _(d=d):
                    filter_copy(p, d).wait_recv()

    def add_xz(p, acc):
        wait_received(p, False)
        def add(layer, v):
            acc[pl.ds(layer * NY, NY), :] = acc[pl.ds(layer * NY, NY), :] + v

        first, second = xr[p, 1, pl.ds(0, NY), :], xr[p, 1, pl.ds(NY, NY), :]
        add(0, first + 2.0 * second)
        add(1, second)
        first, second = xr[p, 0, pl.ds(0, NY), :], xr[p, 0, pl.ds(NY, NY), :]
        add(NX - 2, first)
        add(NX - 1, 2.0 * first + second)
        for k in range(GROUPS):
            low, high = [[zr[p, sz, 2 * k + i] for i in range(2)] for sz in (1, 0)]
            edge = {0: 1, GROUPS - 1: 0}.get(k)
            if edge is not None:
                low, high = [[v[i] + xzr[p, edge, sz, i] for i in range(2)] for v, sz in ((low, 1), (high, 0))]
            acc[pl.ds(k * 128, 128), :] = acc[pl.ds(k * 128, 128), :] + z_edges(low, high)

    def add_y(p, acc):
        wait_received(p, True)
        low, high = [[sum([yzr[p, sy, sz, i] for sy in range(2)] + [
            xyzr[p, sx, sy, sz, i] for sx in range(2) for sy in range(2)]) for i in range(2)] for sz in (1, 0)]
        turned = z_edges(low, high)
        at = {}
        for sy in range(2):
            for n in range(2):
                center = yr[p, sy, n]
                up, down = [[xyr[p, sx, sy, 2 * n + i] for i in range(2)] for sx in (1, 0)]
                at[sy, n] = jnp.concatenate([
                    center[:8] + rows_at({0: up[0], 1: up[1]}), center[8:16],
                    center[16:] + rows_at({6: down[0], 7: down[1]})], 0)
        for n, (row, v) in enumerate((
                (0, at[1, 0] + 2.0 * at[1, 1]), (1, at[1, 1]), (NY - 2, at[0, 0]), (NY - 1, 2.0 * at[0, 0] + at[0, 1]))):
            place = pl.ds(row, NX, stride=NY)
            acc[place, :] = acc[place, :] + v + turned[n * 32:n * 32 + NX]

    load_density.wait()
    local_filter(0, acc)
    load_nodes.wait()

    def first_columns(v):
        lane = iota(v[0].shape, 1)
        return jnp.where(lane == 0, v[0], jnp.where(
            lane == 1, pltpu.roll(v[1], 1, 1), jnp.where(lane == 2, pltpu.roll(v[2], 2, 1), 0.0)))

    for m in range(3):
        dys[m] = nodes[m, pl.ds(0, NX, stride=NY), :]
        dxys[m] = dys[m, pl.ds(0, 1), :]
    for k in range(GROUPS):
        columns = first_columns([nodes[m, pl.ds(k * 128, 128), :] for m in range(3)])
        turned = columns.T[0:8]
        for m in range(3):
            dzs[3 * k + m] = turned[m:m + 1]
        if k == 0:
            m6[pl.ds(0, NY), :] = columns[:NY]
    m6[pl.ds(NY, NX), :] = first_columns([dys[m] for m in range(3)])
    turned = m6[...].T[0:8]
    lane8 = iota((8, 128), 1)
    for target, tile in (
            (dxzs, jnp.where(lane8 < NY, turned, 0.0)),
            (dyzs, jnp.where(jnp.logical_and(lane8 >= NY, lane8 < NY + NX), turned, 0.0)),
            (dxyzs, jnp.where(lane8 == NY + NX, pltpu.roll(turned, NY + NX, 1), 0.0))):
        for m in range(3):
            target[m] = tile[m:m + 1]

    pl.semaphore_wait(barrier, waits)
    for d in LOWER:
        @pl.when(inside(d))
        def _(d=d):
            lower_copy(d).start()
    send_filter(0)

    def wait_lower(along_y):
        for d in LOWER:
            if bool(d[1]) == along_y:
                @pl.when(inside(tuple(-s for s in d)))
                def _(d=d):
                    lower_copy(d).wait_recv()

    rest = jnp.zeros((120, 128), F32)

    def z_pass(base, count, packed):
        halo = jnp.concatenate([rows_at(dict(enumerate(packed))), rest], 0).T[:count]
        lane = iota(halo.shape, 1)
        out = []
        for m in range(3):
            u = nodes[m, pl.ds(base, count), :]
            up = jnp.where(lane == NZ - 1, pltpu.roll(halo, NZ - 1 - m, 1), pltpu.roll(u, NZ - 1, 1))
            out += [u + up, up - u]
        return out

    wait_lower(False)
    for k in range(GROUPS):
        for n, v in enumerate(z_pass(k * 128, 128, [dzr[3 * k + m] for m in range(3)])):
            for i in range(4):
                sd[n, pl.ds((4 * k + i) * NODE_PAD, NY), :] = v[i * NY:(i + 1) * NY]
    for n, v in enumerate(z_pass(ROWS, NY, [dxzr[m] for m in range(3)])):
        sd[n, pl.ds(NX * NODE_PAD, NY), :] = v

    def yz_terms(i, t):
        base = pl.multiple_of(i * NODE_PAD, 8) + 8 * t
        out = []
        for k in range(6):
            here, above = sd[k, pl.ds(base, 8), :], sd[k, pl.ds(base + 1, 8), :]
            out += [here + above, above - here]
        return out

    square = lambda v: v * v

    def energies(t):
        def element(i, before):
            now = yz_terms(i, t)
            w = []
            for m in range(3):
                (a0, a1, a2, a3), (b0, b1, b2, b3) = now[4 * m:4 * m + 4], before[4 * m:4 * m + 4]
                w.append({100: a0 - b0, 110: a1 - b1, 101: a2 - b2, 111: a3 - b3,
                          10: a1 + b1, 1: a2 + b2, 11: a3 + b3})
            u, v, z = w
            total = (LAME / 16) * square(u[100] + v[10] + z[1])
            total += (LAME / 48) * (square(v[110] + z[101]) + square(u[110] + z[11]) + square(u[101] + v[11]))
            total += (SHEAR / 8) * (square(u[100]) + square(v[10]) + square(z[1]))
            total += (SHEAR / 16) * (
                (square(u[110]) + square(u[101]) + square(v[110])) + (square(v[11]) + square(z[101]) + square(z[11]))
                + (square(u[10] + v[100]) + square(v[1] + z[10]) + square(u[1] + z[100])))
            total += (SHEAR / 48) * (square(u[11] + v[101]) + square(v[101] + z[110]) + square(u[11] + z[110]))
            total += ((LAME + 4 * SHEAR) / 144) * (square(u[111]) + square(v[111]) + square(z[111]))
            energy[pl.ds(pl.multiple_of((i - 1) * NY, NY) + 8 * t, 8), :] = total
            return now

        def pair(n, before):
            return tuple(element(2 * n + 2, element(2 * n + 1, before)))

        lax.fori_loop(0, NX // 2, pair, tuple(yz_terms(0, t)))

    for t in range(NY // 8 - 1):
        energies(t)
    add_xz(0, acc)
    wait_lower(True)
    for m in range(3):
        nodes[m, pl.ds(ROWS + NY + NX, 1), :] = dxyr[m]
    for n, v in enumerate(z_pass(ROWS + NY, NY, [pltpu.roll(dyzr[m] + dxyzr[m], 128 - NY, 1) for m in range(3)])):
        sd[n, pl.ds(NY, NX + 1, stride=NODE_PAD), :] = v[:NX + 1]
    energies(NY // 8 - 1)

    add_y(0, acc)

    def inverse_cover(index, extent):
        end = extent - 1
        return jnp.where(jnp.logical_or(index == 0, index == end), 1.0 / 6.0, jnp.where(
            jnp.logical_or(index == 1, index == end - 1), 1.0 / 8.0, 1.0 / 9.0)).astype(F32)

    inverse_yz = inverse_cover(iota((NY, NZ), 0) + gy * NY, NY * size_y) * inverse_cover(
        iota((NY, NZ), 1) + gz * NZ, NZ * size_z)

    total = jnp.zeros((NY, NZ), F32)
    for i in range(NX):
        inverse = inverse_yz * inverse_cover(gx * NX + i, NX * size_x)
        physical = acc[pl.ds(i * NY, NY), :] * inverse
        product = physical * physical * energy[pl.ds(i * NY, NY), :]
        field[pl.ds((i + 2) * NY, NY), :] = -3.0 * product * inverse
        total = total + physical * product
    total = jnp.sum(total, axis=0, keepdims=True)

    def sum_copy(s, mine, to):
        return remote(part.at[s], part_in.at[s, mine], psend_sem.at[s], precv_sem.at[s], to)

    def sum_wait(sem, s, n):
        whole = part_in.at[s, pl.ds(0, n)]
        pltpu.make_async_copy(whole, whole, sem.at[s]).wait()

    mine = my_z * 2 + my_core
    part[0] = total
    for z, c in column:
        @pl.when(other(z, c))
        def _(z=z, c=c):
            sum_copy(0, mine, at_zc(z, c)).start()
    local_filter(1, out)
    send_filter(1)

    @pl.when(early)
    def _():
        part_in[0, mine] = total
        sum_wait(precv_sem, 0, 2 * count_z - 1)
        partial = jnp.sum(part_in[0, 0:2 * count_z], axis=0)
        here = gz * ring_y + my_y
        part[1] = partial
        part_in[1, here] = partial
        for o in plane:
            sum_copy(1, here, partner_xy(*o)).start()

    add_xz(1, out)
    add_y(1, out)

    for d in DIRECTIONS:
        @pl.when(inside(d))
        def _(d=d):
            for p in range(2):
                filter_copy(p, d).wait_send()
            if d in lower:
                lower_copy(d).wait_send()

    @pl.when(early)
    def _():
        sum_wait(psend_sem, 0, 2 * layers_z - 1)
        sum_wait(psend_sem, 1, len(plane))
        sum_wait(precv_sem, 1, len(plane))
        part[2] = jnp.sum(part_in[1, 0:len(plane) + 1], axis=0)

    def pass_on(z):
        return remote(part.at[2], part_in.at[2, 0], pass_sem.at[z - layers_z], precv_sem.at[2], at_zc(z, my_core))

    for z in serves:
        @pl.when(my_z == served_from(z))
        def _(z=z):
            pass_on(z).start()

    @pl.when(jnp.logical_not(early))
    def _():
        sum_wait(psend_sem, 0, 2 * layers_z)
        if halves > 1:
            sum_wait(precv_sem, 2, 1)
            part[2] = part_in[2, 0]

    total_out[...] = jnp.broadcast_to(jnp.sum(part[2], axis=1, keepdims=True), (8, 128))

    for z in serves:
        @pl.when(my_z == served_from(z))
        def _(z=z):
            pass_on(z).wait_send()


def exchange(mesh, density, displacement):
    sizes = (mesh.shape["gx"], mesh.shape["gy"], mesh.shape["gz"], min(8, mesh.shape["gx"]))
    vmem = lambda *shape: pltpu.VMEM(shape, F32)
    partners = max(sizes[0] // sizes[3] * sizes[1], sizes[3] * sizes[2])
    scratch = [
        vmem((NX + 4) * NY, NZ), vmem(NX * YPAD, NZ), vmem(4 * YPAD, NZ), vmem(ROWS, NZ),
        vmem(128, NZ), vmem(128, NZ), vmem(3, ROWS + 2 * NY, NZ),
        vmem(6, (NX + 1) * NODE_PAD, NZ), vmem(ROWS, NZ)]
    filters = [vmem(2, 2, 2 * NY, NZ), vmem(2, 2, 2, NX, NZ), vmem(2, 2, 2, 4, 1, NZ), vmem(2, 2, 2 * GROUPS, 1, 128),
               vmem(2, 2, 2, 2, 1, 128), vmem(2, 2, 2, 2, 1, 128), vmem(2, 2, 2, 2, 2, 1, 128)]
    scratch += filters + filters
    edges = [vmem(3, 1, NZ), vmem(3 * GROUPS, 1, 128), vmem(3, 1, 128), vmem(3, 1, 128), vmem(3, 1, 128)]
    scratch += [vmem(3, NX, NZ)] + edges + edges + [vmem(128, 128)]
    scratch += [vmem(3, 1, 128), vmem(3, partners, 1, 128)]
    dma = pltpu.SemaphoreType.DMA
    scratch += [dma((2, 27)), dma((2, 27)), dma((8,)), dma((8,)), dma((2,)), dma((3,)), dma((3,)), dma((8,))]
    return pl.pallas_call(
        functools.partial(kernel, sizes),
        out_shape=[jax.ShapeDtypeStruct((ROWS, NZ), F32), jax.ShapeDtypeStruct((8, 128), F32)],
        in_specs=[pl.BlockSpec(memory_space=pltpu.HBM)] * 2,
        out_specs=[pl.BlockSpec(memory_space=pltpu.VMEM)] * 2,
        scratch_shapes=scratch,
        compiler_params=pltpu.CompilerParams(
            collective_id=0, has_side_effects=True, vmem_limit_bytes=56_000_000),
        cost_estimate=pl.CostEstimate(flops=20_000_000, bytes_accessed=2_000_000, transcendentals=0),
    )(density, displacement)


def scale_kernel(elements, field, total, out, mean_out, scaled, mean_ref, sem):
    mean = total[0:1, :] / elements
    mean_ref[...] = mean[:, 0:1]
    inverse = 1.0 / mean
    copies = [pltpu.make_async_copy(mean_ref, mean_out, sem.at[PARTS])]
    copies[0].start()
    for n in range(PARTS):
        part = pl.ds(n * (ROWS // PARTS), ROWS // PARTS)
        scaled[part, :] = field[part, :] * inverse
        copies.append(pltpu.make_async_copy(scaled.at[part], out.at[part], sem.at[n]))
        copies[-1].start()
    for copy in copies:
        copy.wait()


def solution(mesh):
    def shards(displacement, density):
        filtered, total = exchange(mesh, density.reshape(ROWS, NZ), displacement.reshape(3, ROWS, NZ))
        sensitivity, mean = pl.pallas_call(
            functools.partial(scale_kernel, float(ROWS * NZ * mesh.size)),
            out_shape=[jax.ShapeDtypeStruct((ROWS, NZ), F32), jax.ShapeDtypeStruct((1, 1), F32)],
            in_specs=[pl.BlockSpec(memory_space=pltpu.VMEM)] * 2,
            out_specs=[pl.BlockSpec(memory_space=pl.ANY)] * 2,
            scratch_shapes=[
                pltpu.VMEM((ROWS, NZ), F32), pltpu.VMEM((1, 1), F32), pltpu.SemaphoreType.DMA((PARTS + 1,))],
            compiler_params=pltpu.CompilerParams(vmem_limit_bytes=4 * 2**20),
        )(filtered, total)
        return sensitivity.reshape(NX, NY, NZ), mean.reshape(())

    return jax.shard_map(
        shards,
        mesh=mesh,
        in_specs=(P(None, "gx", "gy", "gz"), P("gx", "gy", "gz")),
        out_specs=(P("gx", "gy", "gz"), P()),
        check_vma=False,
    )
```

```python
import functools
import itertools

import jax
import jax.numpy as jnp
from jax import lax
from jax.experimental import pallas as pl
from jax.experimental.pallas import tpu as pltpu
from jax.sharding import PartitionSpec as P

MESH = pl.DeviceIdType.MESH
F32 = jnp.float32
NX, NY, NZ = 24, 32, 128
ROWS = NX * NY
GROUPS = ROWS // 128
YPAD = 48
NODE_PAD = 40
PARTS = 4
LAME = 0.3 / (1.3 * 0.4)
SHEAR = 1.0 / 2.6

DIRECTIONS = sorted((d for d in itertools.product((-1, 0, 1), repeat=3) if any(d)), key=lambda d: (not d[1], -sum(map(abs, d))))
LOWER = [d for d in DIRECTIONS if max(d) <= 0]


def slot(direction):
    return (direction[0] + 1) * 9 + (direction[1] + 1) * 3 + direction[2] + 1


def lower_slot(direction):
    return -(direction[0] * 4 + direction[1] * 2 + direction[2])


def iota(shape, axis):
    return lax.broadcasted_iota(jnp.int32, shape, axis)


def hat_lanes(v):
    lane = iota(v.shape, v.ndim - 1)
    axis = v.ndim - 1

    def moved(step):
        rolled = pltpu.roll(v, step % NZ, axis)
        return jnp.where(lane >= step if step > 0 else lane < NZ + step, rolled, 0.0)

    return 3.0 * v + 2.0 * (moved(1) + moved(-1)) + (moved(2) + moved(-2))


def across(v, axis, size, step, direction):
    place = iota(v.shape, axis) // step
    count = size // step
    if direction > 0:
        two, one = pltpu.roll(v, 2 * step, axis), pltpu.roll(v, step, axis)
        return jnp.where(place == 0, two + 2.0 * one, jnp.where(place == 1, two, 0.0))
    two, one = pltpu.roll(v, size - 2 * step, axis), pltpu.roll(v, size - step, axis)
    return jnp.where(place == count - 1, two + 2.0 * one, jnp.where(place == count - 2, two, 0.0))


def rows_at(places):
    row = iota((8, NZ), 0)
    tile = jnp.zeros((8, NZ), F32)
    for place, value in places.items():
        tile = jnp.where(row == place, jnp.broadcast_to(value, (8, NZ)), tile)
    return tile


def kernel(sizes, density, displacement, out, total_out, *scratch):
    (field, g, b4, acc, rows, corner, nodes, sd, energy,
     xs, ys, xys, zs, xzs, yzs, xyzs, xr, yr, xyr, zr, xzr, yzr, xyzr,
     dys, dxys, dzs, dxzs, dyzs, dxyzs, dxyr, dzr, dxzr, dyzr, dxyzr, m6,
     part, part_in, send_sem, recv_sem, dsend_sem, drecv_sem, load_sem, psend_sem, precv_sem, pass_sem) = scratch
    size_x, size_y, size_z, ring_y = sizes
    gx, gy, gz = (lax.axis_index(a) for a in ("gx", "gy", "gz"))

    def inside(direction):
        ok = []
        for place, step, count in zip((gx, gy, gz), direction, (size_x, size_y, size_z)):
            if step > 0:
                ok.append(place < count - 1)
            elif step < 0:
                ok.append(place > 0)
        return functools.reduce(jnp.logical_and, ok)

    def device(direction):
        return (gx + direction[0], gy + direction[1], gz + direction[2])

    layers_z = size_x // ring_y
    my_y, my_z = lax.rem(gx, ring_y), gx // ring_y + layers_z * (gy // 2)
    my_core = lax.rem(gy, 2)
    count_z = layers_z * (size_y // 2)

    halves = size_y // 2
    early = gy < 2

    def at_zc(z, c):
        return (lax.rem(z, layers_z) * ring_y + my_y, (z // layers_z) * 2 + c, gz)

    def partner_xy(dx, dy):
        x, y = lax.rem(gz + dx, size_z), lax.rem(my_y + dy, ring_y)
        return ((gx // ring_y) * ring_y + y, gy, x)

    server = layers_z - 1 - (my_z - layers_z) // 2
    serves = [(z, c) for z in range(layers_z, count_z) for c in range(2)]

    def serving(z):
        return jnp.logical_and(my_z == layers_z - 1 - (z - layers_z) // 2, my_core == 1)

    column = [(z, c) for z in range(layers_z) for c in range(2)]

    def other(z, c):
        return jnp.logical_or(my_z != z, my_core != c)

    def far_first(counts):
        offs = [o for o in itertools.product(*[range(c) for c in counts]) if any(o)]
        return sorted(offs, key=lambda o: -sum(min(s, c - s) for s, c in zip(o, counts)))

    plane = far_first((size_z, ring_y))

    load_density = pltpu.make_async_copy(density, field.at[pl.ds(2 * NY, ROWS)], load_sem.at[0])
    load_nodes = pltpu.make_async_copy(displacement, nodes.at[:, pl.ds(0, ROWS)], load_sem.at[1])
    load_density.start()
    load_nodes.start()

    barrier = pltpu.get_barrier_semaphore()

    def greet(to):
        pl.semaphore_signal(barrier, inc=1, device_id=to, device_id_type=MESH)

    waits = 0
    for d in DIRECTIONS:
        @pl.when(inside(d))
        def _(d=d):
            greet(device(d))
        waits = waits + inside(d).astype(jnp.int32)

    @pl.when(early)
    def _():
        for z, c in [(z, c) for z in range(count_z) for c in range(2)]:
            @pl.when(other(z, c))
            def _(z=z, c=c):
                greet(at_zc(z, c))
        for o in plane:
            greet(partner_xy(*o))

    if halves > 1:
        @pl.when(jnp.logical_not(early))
        def _():
            greet(at_zc(server, 1))

    served = sum(serving(z).astype(jnp.int32) for z, _ in serves) if serves else 0
    waits = waits + jnp.where(early, 2 * layers_z - 1 + len(plane) + served, 2 * layers_z)

    zero_row = jnp.zeros((8, NZ), F32)

    def zero(ref):
        ref[...] = jnp.zeros(ref.shape, F32)

    received = {}
    for d in DIRECTIONS:
        sx, sy, sz = ((s + 1) // 2 for s in d)
        kind = tuple(bool(s) for s in d)
        received[d] = {
            (True, False, False): lambda p: (xs.at[p, sx], xr.at[p, sx]),
            (False, True, False): lambda p: (ys.at[p, sy], yr.at[p, sy]),
            (True, True, False): lambda p: (xys.at[p, sx, sy], xyr.at[p, sx, sy]),
            (False, False, True): lambda p: (zs.at[p, sz], zr.at[p, sz]),
            (True, False, True): lambda p: (xzs.at[p, sx, sz], xzr.at[p, sx, sz]),
            (False, True, True): lambda p: (yzs.at[p, sy, sz], yzr.at[p, sy, sz]),
            (True, True, True): lambda p: (xyzs.at[p, sx, sy, sz], xyzr.at[p, sx, sy, sz]),
        }[kind]
        received[d] = [received[d](p) for p in range(2)]
    lower = {
        (-1, 0, 0): (nodes.at[:, pl.ds(0, NY)], nodes.at[:, pl.ds(ROWS, NY)]),
        (0, -1, 0): (dys, nodes.at[:, pl.ds(ROWS + NY, NX)]),
        (-1, -1, 0): (dxys, dxyr),
        (0, 0, -1): (dzs, dzr),
        (-1, 0, -1): (dxzs, dxzr),
        (0, -1, -1): (dyzs, dyzr),
        (-1, -1, -1): (dxyzs, dxyzr),
    }

    for d in DIRECTIONS:
        @pl.when(jnp.logical_not(inside(tuple(-s for s in d))))
        def _(d=d):
            for p in range(2):
                zero(received[d][p][1])
            if d in lower:
                zero(lower[d][1])

    def remote(source, target, send, recv, to):
        return pltpu.make_async_remote_copy(
            src_ref=source, dst_ref=target, send_sem=send, recv_sem=recv, device_id=to, device_id_type=MESH)

    def filter_copy(p, d):
        source, target = received[d][p]
        return remote(source, target, send_sem.at[p, slot(d)], recv_sem.at[p, slot(d)], device(d))

    def lower_copy(d):
        source, target = lower[d]
        return remote(source, target, dsend_sem.at[lower_slot(d)], drecv_sem.at[lower_slot(d)], device(d))

    for margin in (0, NY, (NX + 2) * NY, (NX + 3) * NY):
        field[pl.ds(margin, NY), :] = jnp.zeros((NY, NZ), F32)

    for i in range(NX):
        g[pl.ds(i * YPAD, 8), :] = zero_row
        g[pl.ds(i * YPAD + 40, 8), :] = zero_row
    for i in range(4):
        b4[pl.ds(i * YPAD, 8), :] = zero_row
        b4[pl.ds(i * YPAD + 40, 8), :] = zero_row
    zero(rows)
    zero(corner)
    zero(m6)

    middle = jnp.zeros((112, 128), F32)

    def hat_rows(ref, base):
        at = [ref[pl.ds(base + 6 + k, NY), :] for k in range(5)]
        return 3.0 * at[2] + 2.0 * (at[1] + at[3]) + (at[0] + at[4])

    def store_pair(ref, tile, first):
        ref[0] = tile[first:first + 1]
        ref[1] = tile[first + 1:first + 2]

    def z_edges(low, high):
        return jnp.concatenate([
            rows_at({0: low[0] + 2.0 * low[1], 1: low[1]}), middle,
            rows_at({6: high[0], 7: 2.0 * high[0] + high[1]})], 0).T

    def local_filter(p, ref):
        for n, layer in enumerate((0, 1, NX - 2, NX - 1)):
            b4[pl.ds(n * YPAD + 8, NY), :] = field[pl.ds((layer + 2) * NY, NY), :]
        faces = [hat_rows(b4, n * YPAD) for n in range(4)]
        for n in range(4):
            xs[p, n // 2, pl.ds((n % 2) * NY, NY), :] = hat_lanes(faces[n])
        turned = jnp.concatenate(faces, 0).T
        for sz, part_z in enumerate((turned[0:8], turned[120:128])):
            for sx in range(2):
                store_pair(xzs.at[p, sx, sz], across(part_z, 1, 128, 32, 2 * sx - 1), 6 * sz)

        for t in range(NY // 8):
            at = [field[pl.ds(i * NY + 8 * t, 8), :] for i in range(NX + 4)]
            for i in range(NX):
                g[pl.ds(i * YPAD + 8 + 8 * t, 8), :] = (
                    3.0 * at[i + 2] + 2.0 * (at[i + 1] + at[i + 3]) + (at[i] + at[i + 4]))

        for n, row in enumerate((0, 1, NY - 2, NY - 1)):
            edge = g[pl.ds(8 + row, NX, stride=YPAD), :]
            rows[pl.ds(n * 32, NX), :] = edge
            ys[p, n // 2, n % 2] = hat_lanes(edge)
            raw = field[pl.ds(2 * NY + row, NX, stride=NY), :]
            up, down = across(raw[NX - 8:], 0, 8, 1, 1), across(raw[:8], 0, 8, 1, -1)
            corner[pl.ds(n * 32, 8), :] = up
            corner[pl.ds(n * 32 + NX - 8, 8), :] = down
            store_pair(xys.at[p, 1, n // 2, pl.ds(2 * (n % 2), 2)], hat_lanes(up), 0)
            store_pair(xys.at[p, 0, n // 2, pl.ds(2 * (n % 2), 2)], hat_lanes(down), 6)
        turned = rows[...].T
        for sz, part_z in enumerate((turned[0:8], turned[120:128])):
            for sy in range(2):
                store_pair(yzs.at[p, sy, sz], across(part_z, 1, 128, 32, 2 * sy - 1), 6 * sz)
        turned = corner[...].T
        lane = lax.rem(iota((8, 128), 1), 32)
        for sz, part_z in enumerate((turned[0:8], turned[120:128])):
            for sy in range(2):
                both = across(part_z, 1, 128, 32, 2 * sy - 1)
                store_pair(xyzs.at[p, 1, sy, sz], jnp.where(lane < 8, both, 0.0), 6 * sz)
                store_pair(xyzs.at[p, 0, sy, sz], jnp.where(lane < 8, 0.0, both), 6 * sz)

        for k in range(GROUPS):
            v = jnp.concatenate([hat_rows(g, (4 * k + n) * YPAD) for n in range(4)], 0)
            ref[pl.ds(k * 128, 128), :] = hat_lanes(v)
            turned = v.T
            store_pair(zs.at[p, 0, pl.ds(2 * k, 2)], turned[0:8], 0)
            store_pair(zs.at[p, 1, pl.ds(2 * k, 2)], turned[120:128], 6)

    def send_filter(p, along_y, when=None, faces=(True, False)):
        for d in DIRECTIONS:
            if d[1] == along_y and (d == (0, along_y, 0)) in faces:
                go = inside(d) if when is None else jnp.logical_and(inside(d), when)

                @pl.when(go)
                def _(d=d):
                    filter_copy(p, d).start()

    def send_lower(along_y, when=None):
        for d in sorted(LOWER, key=lambda d: (d[0] != 0 if along_y == 0 else 0, -sum(map(abs, d)))):
            if d[1] == along_y:
                go = inside(d) if when is None else jnp.logical_and(inside(d), when)

                @pl.when(go)
                def _(d=d):
                    lower_copy(d).start()

    up_far, down_far = my_core == 1, my_core == 0

    def wait_received(p, along_y):
        for d in reversed(DIRECTIONS):
            if bool(d[1]) == along_y:
                @pl.when(inside(tuple(-s for s in d)))
                def _(d=d):
                    filter_copy(p, d).wait_recv()

    def add_xz(p, acc):
        wait_received(p, False)
        def add(layer, v):
            acc[pl.ds(layer * NY, NY), :] = acc[pl.ds(layer * NY, NY), :] + v

        first, second = xr[p, 1, pl.ds(0, NY), :], xr[p, 1, pl.ds(NY, NY), :]
        add(0, first + 2.0 * second)
        add(1, second)
        first, second = xr[p, 0, pl.ds(0, NY), :], xr[p, 0, pl.ds(NY, NY), :]
        add(NX - 2, first)
        add(NX - 1, 2.0 * first + second)
        for k in range(GROUPS):
            low, high = [[zr[p, sz, 2 * k + i] for i in range(2)] for sz in (1, 0)]
            edge = {0: 1, GROUPS - 1: 0}.get(k)
            if edge is not None:
                low, high = [[v[i] + xzr[p, edge, sz, i] for i in range(2)] for v, sz in ((low, 1), (high, 0))]
            acc[pl.ds(k * 128, 128), :] = acc[pl.ds(k * 128, 128), :] + z_edges(low, high)

    def add_y(p, acc):
        wait_received(p, True)
        low, high = [[sum([yzr[p, sy, sz, i] for sy in range(2)] + [
            xyzr[p, sx, sy, sz, i] for sx in range(2) for sy in range(2)]) for i in range(2)] for sz in (1, 0)]
        turned = z_edges(low, high)
        at = {}
        for sy in range(2):
            for n in range(2):
                center = yr[p, sy, n]
                up, down = [[xyr[p, sx, sy, 2 * n + i] for i in range(2)] for sx in (1, 0)]
                at[sy, n] = jnp.concatenate([
                    center[:8] + rows_at({0: up[0], 1: up[1]}), center[8:16],
                    center[16:] + rows_at({6: down[0], 7: down[1]})], 0)
        for n, (row, v) in enumerate((
                (0, at[1, 0] + 2.0 * at[1, 1]), (1, at[1, 1]), (NY - 2, at[0, 0]), (NY - 1, 2.0 * at[0, 0] + at[0, 1]))):
            place = pl.ds(row, NX, stride=NY)
            acc[place, :] = acc[place, :] + v + turned[n * 32:n * 32 + NX]

    load_density.wait()
    local_filter(0, acc)
    load_nodes.wait()

    def first_columns(v):
        lane = iota(v[0].shape, 1)
        return jnp.where(lane == 0, v[0], jnp.where(
            lane == 1, pltpu.roll(v[1], 1, 1), jnp.where(lane == 2, pltpu.roll(v[2], 2, 1), 0.0)))

    for m in range(3):
        dys[m] = nodes[m, pl.ds(0, NX, stride=NY), :]
        dxys[m] = dys[m, pl.ds(0, 1), :]
    for k in range(GROUPS):
        columns = first_columns([nodes[m, pl.ds(k * 128, 128), :] for m in range(3)])
        turned = columns.T[0:8]
        for m in range(3):
            dzs[3 * k + m] = turned[m:m + 1]
        if k == 0:
            m6[pl.ds(0, NY), :] = columns[:NY]
    m6[pl.ds(NY, NX), :] = first_columns([dys[m] for m in range(3)])
    turned = m6[...].T[0:8]
    lane8 = iota((8, 128), 1)
    for target, tile in (
            (dxzs, jnp.where(lane8 < NY, turned, 0.0)),
            (dyzs, jnp.where(jnp.logical_and(lane8 >= NY, lane8 < NY + NX), turned, 0.0)),
            (dxyzs, jnp.where(lane8 == NY + NX, pltpu.roll(turned, NY + NX, 1), 0.0))):
        for m in range(3):
            target[m] = tile[m:m + 1]

    pl.semaphore_wait(barrier, waits)
    send_filter(0, 1, up_far, (False,))
    send_lower(-1, down_far)
    send_filter(0, -1, down_far)
    send_lower(0)
    send_filter(0, 1, up_far, (True,))
    send_filter(0, 0)
    send_lower(-1, up_far)
    send_filter(0, -1, up_far)
    send_filter(0, 1, down_far)

    def wait_lower(*directions):
        for d in LOWER:
            if d in directions:
                @pl.when(inside(tuple(-s for s in d)))
                def _(d=d):
                    lower_copy(d).wait_recv()

    rest = jnp.zeros((120, 128), F32)

    def z_pass(base, count, packed):
        halo = jnp.concatenate([rows_at(dict(enumerate(packed))), rest], 0).T[:count]
        lane = iota(halo.shape, 1)
        out = []
        for m in range(3):
            u = nodes[m, pl.ds(base, count), :]
            up = jnp.where(lane == NZ - 1, pltpu.roll(halo, NZ - 1 - m, 1), pltpu.roll(u, NZ - 1, 1))
            out += [u + up, up - u]
        return out

    wait_lower((0, 0, -1))
    for k in range(GROUPS):
        for n, v in enumerate(z_pass(k * 128, 128, [dzr[3 * k + m] for m in range(3)])):
            for i in range(4):
                sd[n, pl.ds((4 * k + i) * NODE_PAD, NY), :] = v[i * NY:(i + 1) * NY]

    def yz_terms(i, t):
        base = pl.multiple_of(i * NODE_PAD, 8) + 8 * t
        out = []
        for k in range(6):
            here, above = sd[k, pl.ds(base, 8), :], sd[k, pl.ds(base + 1, 8), :]
            out += [here + above, above - here]
        return out

    square = lambda v: v * v

    def energies(t, first, end):
        def element(i, before):
            now = yz_terms(i, t)
            w = []
            for m in range(3):
                (a0, a1, a2, a3), (b0, b1, b2, b3) = now[4 * m:4 * m + 4], before[4 * m:4 * m + 4]
                w.append({100: a0 - b0, 110: a1 - b1, 101: a2 - b2, 111: a3 - b3,
                          10: a1 + b1, 1: a2 + b2, 11: a3 + b3})
            u, v, z = w
            total = (LAME / 16) * square(u[100] + v[10] + z[1])
            total += (LAME / 48) * (square(v[110] + z[101]) + square(u[110] + z[11]) + square(u[101] + v[11]))
            total += (SHEAR / 8) * (square(u[100]) + square(v[10]) + square(z[1]))
            total += (SHEAR / 16) * (
                (square(u[110]) + square(u[101]) + square(v[110])) + (square(v[11]) + square(z[101]) + square(z[11]))
                + (square(u[10] + v[100]) + square(v[1] + z[10]) + square(u[1] + z[100])))
            total += (SHEAR / 48) * (square(u[11] + v[101]) + square(v[101] + z[110]) + square(u[11] + z[110]))
            total += ((LAME + 4 * SHEAR) / 144) * (square(u[111]) + square(v[111]) + square(z[111]))
            energy[pl.ds(pl.multiple_of((i - 1) * NY, NY) + 8 * t, 8), :] = total
            return now

        def pair(n, before):
            return tuple(element(2 * n + 2, element(2 * n + 1, before)))

        lax.fori_loop(first, end, pair, tuple(yz_terms(2 * first, t)))

    for t in range(NY // 8 - 1):
        energies(t, 0, NX // 2 - 1)
    wait_lower((-1, 0, 0), (-1, 0, -1))
    for n, v in enumerate(z_pass(ROWS, NY, [dxzr[m] for m in range(3)])):
        sd[n, pl.ds(NX * NODE_PAD, NY), :] = v
    for t in range(NY // 8 - 1):
        energies(t, NX // 2 - 1, NX // 2)
    add_xz(0, acc)
    wait_lower(*[d for d in LOWER if d[1]])
    for m in range(3):
        nodes[m, pl.ds(ROWS + NY + NX, 1), :] = dxyr[m]
    for n, v in enumerate(z_pass(ROWS + NY, NY, [pltpu.roll(dyzr[m] + dxyzr[m], 128 - NY, 1) for m in range(3)])):
        sd[n, pl.ds(NY, NX + 1, stride=NODE_PAD), :] = v[:NX + 1]
    energies(NY // 8 - 1, 0, NX // 2)

    def inverse_cover(index, extent):
        end = extent - 1
        return jnp.where(jnp.logical_or(index == 0, index == end), 1.0 / 6.0, jnp.where(
            jnp.logical_or(index == 1, index == end - 1), 1.0 / 8.0, 1.0 / 9.0)).astype(F32)

    inverse_yz = inverse_cover(iota((NY, NZ), 0) + gy * NY, NY * size_y) * inverse_cover(
        iota((NY, NZ), 1) + gz * NZ, NZ * size_z)

    def weigh(physical, energies_, inverse):
        product = physical * physical * energies_
        return -3.0 * product * inverse, physical * product

    y_rows = (0, 1, NY - 2, NY - 1)
    total = jnp.zeros((NY, NZ), F32)
    for i in range(NX):
        inverse = inverse_yz * inverse_cover(gx * NX + i, NX * size_x)
        slope, term = weigh(acc[pl.ds(i * NY, NY), :] * inverse, energy[pl.ds(i * NY, NY), :], inverse)
        field[pl.ds((i + 2) * NY, NY), :] = slope
        total = total + term
    row = iota((NY, NZ), 0)
    inner = jnp.logical_and(row >= 2, row < NY - 2)
    total = jnp.sum(jnp.where(inner, total, 0.0), axis=0, keepdims=True)

    inverse_x = inverse_cover(iota((NX, NZ), 0) + gx * NX, NX * size_x)
    inverses = [inverse_x * inverse_yz[row:row + 1] for row in y_rows]
    energy_rows = [energy[pl.ds(row, NX, stride=NY), :] for row in y_rows]
    add_y(0, acc)
    rows_total = jnp.zeros((NX, NZ), F32)
    for n, row in enumerate(y_rows):
        slope, term = weigh(acc[pl.ds(row, NX, stride=NY), :] * inverses[n], energy_rows[n], inverses[n])
        field[pl.ds(2 * NY + row, NX, stride=NY), :] = slope
        rows_total = rows_total + term
    total = total + jnp.sum(rows_total, axis=0, keepdims=True)

    def sum_copy(s, mine, to):
        return remote(part.at[s], part_in.at[s, mine], psend_sem.at[s], precv_sem.at[s], to)

    def sum_wait(sem, s, n):
        whole = part_in.at[s, pl.ds(0, n)]
        pltpu.make_async_copy(whole, whole, sem.at[s]).wait()

    mine = my_z * 2 + my_core
    part[0] = total
    for z, c in column:
        @pl.when(other(z, c))
        def _(z=z, c=c):
            sum_copy(0, mine, at_zc(z, c)).start()
    local_filter(1, out)
    for along_y in (1, 0, -1):
        send_filter(1, along_y)

    @pl.when(early)
    def _():
        part_in[0, mine] = total
        sum_wait(precv_sem, 0, 2 * count_z - 1)
        partial = jnp.sum(part_in[0, 0:2 * count_z], axis=0)
        here = gz * ring_y + my_y
        part[1] = partial
        part_in[1, here] = partial
        for o in plane:
            sum_copy(1, here, partner_xy(*o)).start()

    add_xz(1, out)
    add_y(1, out)

    for d in DIRECTIONS:
        @pl.when(inside(d))
        def _(d=d):
            for p in range(2):
                filter_copy(p, d).wait_send()
            if d in lower:
                lower_copy(d).wait_send()

    @pl.when(early)
    def _():
        sum_wait(psend_sem, 0, 2 * layers_z - 1)
        sum_wait(psend_sem, 1, len(plane))
        sum_wait(precv_sem, 1, len(plane))
        part[2] = jnp.sum(part_in[1, 0:len(plane) + 1], axis=0)

    def pass_on(z, c):
        return remote(
            part.at[2], part_in.at[2, 0], pass_sem.at[2 * (z - layers_z) + c], precv_sem.at[2], at_zc(z, c))

    for z, c in serves:
        @pl.when(serving(z))
        def _(z=z, c=c):
            pass_on(z, c).start()

    @pl.when(jnp.logical_not(early))
    def _():
        sum_wait(psend_sem, 0, 2 * layers_z)
        if halves > 1:
            sum_wait(precv_sem, 2, 1)
            part[2] = part_in[2, 0]

    total_out[...] = jnp.broadcast_to(jnp.sum(part[2], axis=1, keepdims=True), (8, 128))

    for z, c in serves:
        @pl.when(serving(z))
        def _(z=z, c=c):
            pass_on(z, c).wait_send()


def exchange(mesh, density, displacement):
    sizes = (mesh.shape["gx"], mesh.shape["gy"], mesh.shape["gz"], min(8, mesh.shape["gx"]))
    vmem = lambda *shape: pltpu.VMEM(shape, F32)
    partners = max(sizes[0] // sizes[3] * sizes[1], sizes[3] * sizes[2])
    scratch = [
        vmem((NX + 4) * NY, NZ), vmem(NX * YPAD, NZ), vmem(4 * YPAD, NZ), vmem(ROWS, NZ),
        vmem(128, NZ), vmem(128, NZ), vmem(3, ROWS + 2 * NY, NZ),
        vmem(6, (NX + 1) * NODE_PAD, NZ), vmem(ROWS, NZ)]
    filters = [vmem(2, 2, 2 * NY, NZ), vmem(2, 2, 2, NX, NZ), vmem(2, 2, 2, 4, 1, NZ), vmem(2, 2, 2 * GROUPS, 1, 128),
               vmem(2, 2, 2, 2, 1, 128), vmem(2, 2, 2, 2, 1, 128), vmem(2, 2, 2, 2, 2, 1, 128)]
    scratch += filters + filters
    edges = [vmem(3, 1, NZ), vmem(3 * GROUPS, 1, 128), vmem(3, 1, 128), vmem(3, 1, 128), vmem(3, 1, 128)]
    scratch += [vmem(3, NX, NZ)] + edges + edges + [vmem(128, 128)]
    scratch += [vmem(3, 1, 128), vmem(3, partners, 1, 128)]
    dma = pltpu.SemaphoreType.DMA
    scratch += [dma((2, 27)), dma((2, 27)), dma((8,)), dma((8,)), dma((2,)), dma((3,)), dma((3,)), dma((8,))]
    return pl.pallas_call(
        functools.partial(kernel, sizes),
        out_shape=[jax.ShapeDtypeStruct((ROWS, NZ), F32), jax.ShapeDtypeStruct((8, 128), F32)],
        in_specs=[pl.BlockSpec(memory_space=pltpu.HBM)] * 2,
        out_specs=[pl.BlockSpec(memory_space=pltpu.VMEM)] * 2,
        scratch_shapes=scratch,
        compiler_params=pltpu.CompilerParams(
            collective_id=0, has_side_effects=True, vmem_limit_bytes=56_000_000),
        cost_estimate=pl.CostEstimate(flops=20_000_000, bytes_accessed=2_000_000, transcendentals=0),
    )(density, displacement)


def scale_kernel(elements, field, total, out, mean_out, scaled, mean_ref, sem):
    mean = total[0:1, :] / elements
    mean_ref[...] = mean[:, 0:1]
    inverse = 1.0 / mean
    copies = [pltpu.make_async_copy(mean_ref, mean_out, sem.at[PARTS])]
    copies[0].start()
    for n in range(PARTS):
        part = pl.ds(n * (ROWS // PARTS), ROWS // PARTS)
        scaled[part, :] = field[part, :] * inverse
        copies.append(pltpu.make_async_copy(scaled.at[part], out.at[part], sem.at[n]))
        copies[-1].start()
    for copy in copies:
        copy.wait()


def solution(mesh):
    def shards(displacement, density):
        filtered, total = exchange(mesh, density.reshape(ROWS, NZ), displacement.reshape(3, ROWS, NZ))
        sensitivity, mean = pl.pallas_call(
            functools.partial(scale_kernel, float(ROWS * NZ * mesh.size)),
            out_shape=[jax.ShapeDtypeStruct((ROWS, NZ), F32), jax.ShapeDtypeStruct((1, 1), F32)],
            in_specs=[pl.BlockSpec(memory_space=pltpu.VMEM)] * 2,
            out_specs=[pl.BlockSpec(memory_space=pl.ANY)] * 2,
            scratch_shapes=[
                pltpu.VMEM((ROWS, NZ), F32), pltpu.VMEM((1, 1), F32), pltpu.SemaphoreType.DMA((PARTS + 1,))],
            compiler_params=pltpu.CompilerParams(vmem_limit_bytes=4 * 2**20),
        )(filtered, total)
        return sensitivity.reshape(NX, NY, NZ), mean.reshape(())

    return jax.shard_map(
        shards,
        mesh=mesh,
        in_specs=(P(None, "gx", "gy", "gz"), P("gx", "gy", "gz")),
        out_specs=(P("gx", "gy", "gz"), P()),
        check_vma=False,
    )
```

```python
import functools
import itertools

import jax
import jax.numpy as jnp
from jax import lax
from jax.experimental import pallas as pl
from jax.experimental.pallas import tpu as pltpu
from jax.sharding import PartitionSpec as P

MESH = pl.DeviceIdType.MESH
F32 = jnp.float32
NX, NY, NZ = 24, 32, 128
ROWS = NX * NY
GROUPS = ROWS // 128
YPAD = 48
NODE_PAD = 40
PARTS = 4
LAME = 0.3 / (1.3 * 0.4)
SHEAR = 1.0 / 2.6

DIRECTIONS = sorted((d for d in itertools.product((-1, 0, 1), repeat=3) if any(d)), key=lambda d: (not d[1], -sum(map(abs, d))))
LOWER = [d for d in DIRECTIONS if max(d) <= 0]


def slot(direction):
    return (direction[0] + 1) * 9 + (direction[1] + 1) * 3 + direction[2] + 1


def lower_slot(direction):
    return -(direction[0] * 4 + direction[1] * 2 + direction[2])


def iota(shape, axis):
    return lax.broadcasted_iota(jnp.int32, shape, axis)


def hat_lanes(v):
    lane = iota(v.shape, v.ndim - 1)
    axis = v.ndim - 1

    def moved(step):
        rolled = pltpu.roll(v, step % NZ, axis)
        return jnp.where(lane >= step if step > 0 else lane < NZ + step, rolled, 0.0)

    return 3.0 * v + 2.0 * (moved(1) + moved(-1)) + (moved(2) + moved(-2))


def across(v, axis, size, step, direction):
    place = iota(v.shape, axis) // step
    count = size // step
    if direction > 0:
        two, one = pltpu.roll(v, 2 * step, axis), pltpu.roll(v, step, axis)
        return jnp.where(place == 0, two + 2.0 * one, jnp.where(place == 1, two, 0.0))
    two, one = pltpu.roll(v, size - 2 * step, axis), pltpu.roll(v, size - step, axis)
    return jnp.where(place == count - 1, two + 2.0 * one, jnp.where(place == count - 2, two, 0.0))


def rows_at(places):
    row = iota((8, NZ), 0)
    tile = jnp.zeros((8, NZ), F32)
    for place, value in places.items():
        tile = jnp.where(row == place, jnp.broadcast_to(value, (8, NZ)), tile)
    return tile


def kernel(sizes, density, displacement, out, total_out, *scratch):
    (field, g, b4, acc, rows, corner, nodes, sd, energy,
     xs, ys, xys, zs, xzs, yzs, xyzs, xr, yr, xyr, zr, xzr, yzr, xyzr,
     dys, dxys, dzs, dxzs, dyzs, dxyzs, dxyr, dzr, dxzr, dyzr, dxyzr, m6,
     part, part_in, send_sem, recv_sem, dsend_sem, drecv_sem, load_sem, psend_sem, precv_sem, pass_sem) = scratch
    size_x, size_y, size_z, ring_y = sizes
    gx, gy, gz = (lax.axis_index(a) for a in ("gx", "gy", "gz"))

    def inside(direction):
        ok = []
        for place, step, count in zip((gx, gy, gz), direction, (size_x, size_y, size_z)):
            if step > 0:
                ok.append(place < count - 1)
            elif step < 0:
                ok.append(place > 0)
        return functools.reduce(jnp.logical_and, ok)

    def device(direction):
        return (gx + direction[0], gy + direction[1], gz + direction[2])

    layers_z = size_x // ring_y
    my_y, my_z = lax.rem(gx, ring_y), gx // ring_y + layers_z * (gy // 2)
    my_core = lax.rem(gy, 2)
    count_z = layers_z * (size_y // 2)

    halves = size_y // 2
    early = gy < 2

    def at_zc(z, c):
        return (lax.rem(z, layers_z) * ring_y + my_y, (z // layers_z) * 2 + c, gz)

    def partner_xy(dx, dy):
        x, y = lax.rem(gz + dx, size_z), lax.rem(my_y + dy, ring_y)
        return ((gx // ring_y) * ring_y + y, gy, x)

    server = layers_z - 1 - (my_z - layers_z) // 2
    serves = [(z, c) for z in range(layers_z, count_z) for c in range(2)]

    def serving(z):
        return jnp.logical_and(my_z == layers_z - 1 - (z - layers_z) // 2, my_core == 1)

    column = [(z, c) for z in range(layers_z) for c in range(2)]

    def other(z, c):
        return jnp.logical_or(my_z != z, my_core != c)

    def far_first(counts):
        offs = [o for o in itertools.product(*[range(c) for c in counts]) if any(o)]
        return sorted(offs, key=lambda o: -sum(min(s, c - s) for s, c in zip(o, counts)))

    plane = far_first((size_z, ring_y))

    load_density = pltpu.make_async_copy(density, field.at[pl.ds(2 * NY, ROWS)], load_sem.at[0])
    load_nodes = pltpu.make_async_copy(displacement, nodes.at[:, pl.ds(0, ROWS)], load_sem.at[1])
    load_density.start()
    load_nodes.start()

    barrier = pltpu.get_barrier_semaphore()

    def greet(to):
        pl.semaphore_signal(barrier, inc=1, device_id=to, device_id_type=MESH)

    waits = 0
    for d in DIRECTIONS:
        @pl.when(inside(d))
        def _(d=d):
            greet(device(d))
        waits = waits + inside(d).astype(jnp.int32)

    @pl.when(early)
    def _():
        for z, c in [(z, c) for z in range(count_z) for c in range(2)]:
            @pl.when(other(z, c))
            def _(z=z, c=c):
                greet(at_zc(z, c))
        for o in plane:
            greet(partner_xy(*o))

    if halves > 1:
        @pl.when(jnp.logical_not(early))
        def _():
            greet(at_zc(server, 1))

    served = sum(serving(z).astype(jnp.int32) for z, _ in serves) if serves else 0
    waits = waits + jnp.where(early, 2 * layers_z - 1 + len(plane) + served, 2 * layers_z)

    zero_row = jnp.zeros((8, NZ), F32)

    def zero(ref):
        ref[...] = jnp.zeros(ref.shape, F32)

    received = {}
    for d in DIRECTIONS:
        sx, sy, sz = ((s + 1) // 2 for s in d)
        kind = tuple(bool(s) for s in d)
        received[d] = {
            (True, False, False): lambda p: (xs.at[p, sx], xr.at[p, sx]),
            (False, True, False): lambda p: (ys.at[p, sy], yr.at[p, sy]),
            (True, True, False): lambda p: (xys.at[p, sx, sy], xyr.at[p, sx, sy]),
            (False, False, True): lambda p: (zs.at[p, sz], zr.at[p, sz]),
            (True, False, True): lambda p: (xzs.at[p, sx, sz], xzr.at[p, sx, sz]),
            (False, True, True): lambda p: (yzs.at[p, sy, sz], yzr.at[p, sy, sz]),
            (True, True, True): lambda p: (xyzs.at[p, sx, sy, sz], xyzr.at[p, sx, sy, sz]),
        }[kind]
        received[d] = [received[d](p) for p in range(2)]
    lower = {
        (-1, 0, 0): (nodes.at[:, pl.ds(0, NY)], nodes.at[:, pl.ds(ROWS, NY)]),
        (0, -1, 0): (dys, nodes.at[:, pl.ds(ROWS + NY, NX)]),
        (-1, -1, 0): (dxys.at[pl.ds(0, 3)], dxyr.at[pl.ds(0, 3)]),
        (0, 0, -1): (dzs.at[pl.ds(0, 3 * GROUPS)], dzr.at[pl.ds(0, 3 * GROUPS)]),
        (-1, 0, -1): (dxzs.at[pl.ds(0, 3)], dxzr.at[pl.ds(0, 3)]),
        (0, -1, -1): (dyzs.at[pl.ds(0, 3)], dyzr.at[pl.ds(0, 3)]),
        (-1, -1, -1): (dxyzs.at[pl.ds(0, 3)], dxyzr.at[pl.ds(0, 3)]),
    }

    for d in DIRECTIONS:
        @pl.when(jnp.logical_not(inside(tuple(-s for s in d))))
        def _(d=d):
            for p in range(2):
                zero(received[d][p][1])
            if d in lower:
                zero(lower[d][1])

    def remote(source, target, send, recv, to):
        return pltpu.make_async_remote_copy(
            src_ref=source, dst_ref=target, send_sem=send, recv_sem=recv, device_id=to, device_id_type=MESH)

    def filter_copy(p, d):
        source, target = received[d][p]
        return remote(source, target, send_sem.at[p, slot(d)], recv_sem.at[p, slot(d)], device(d))

    def lower_copy(d):
        source, target = lower[d]
        return remote(source, target, dsend_sem.at[lower_slot(d)], drecv_sem.at[lower_slot(d)], device(d))

    for margin in (0, NY, (NX + 2) * NY, (NX + 3) * NY):
        field[pl.ds(margin, NY), :] = jnp.zeros((NY, NZ), F32)

    for i in range(NX):
        g[pl.ds(i * YPAD, 8), :] = zero_row
        g[pl.ds(i * YPAD + 40, 8), :] = zero_row
    for i in range(4):
        b4[pl.ds(i * YPAD, 8), :] = zero_row
        b4[pl.ds(i * YPAD + 40, 8), :] = zero_row
    zero(rows)
    zero(corner)
    zero(m6)

    middle = jnp.zeros((112, 128), F32)

    def hat_rows(ref, base):
        at = [ref[pl.ds(base + 6 + k, NY), :] for k in range(5)]
        return 3.0 * at[2] + 2.0 * (at[1] + at[3]) + (at[0] + at[4])

    def store_pair(ref, tile, first):
        ref[0] = tile[first:first + 1]
        ref[1] = tile[first + 1:first + 2]

    def z_edges(low, high):
        return jnp.concatenate([
            rows_at({0: low[0] + 2.0 * low[1], 1: low[1]}), middle,
            rows_at({6: high[0], 7: 2.0 * high[0] + high[1]})], 0).T

    def local_filter(p, ref):
        for n, layer in enumerate((0, 1, NX - 2, NX - 1)):
            b4[pl.ds(n * YPAD + 8, NY), :] = field[pl.ds((layer + 2) * NY, NY), :]
        faces = [hat_rows(b4, n * YPAD) for n in range(4)]
        for n in range(4):
            xs[p, n // 2, pl.ds((n % 2) * NY, NY), :] = hat_lanes(faces[n])
        turned = jnp.concatenate(faces, 0).T
        for sz, part_z in enumerate((turned[0:8], turned[120:128])):
            for sx in range(2):
                store_pair(xzs.at[p, sx, sz], across(part_z, 1, 128, 32, 2 * sx - 1), 6 * sz)

        for t in range(NY // 8):
            at = [field[pl.ds(i * NY + 8 * t, 8), :] for i in range(NX + 4)]
            for i in range(NX):
                g[pl.ds(i * YPAD + 8 + 8 * t, 8), :] = (
                    3.0 * at[i + 2] + 2.0 * (at[i + 1] + at[i + 3]) + (at[i] + at[i + 4]))

        for n, row in enumerate((0, 1, NY - 2, NY - 1)):
            edge = g[pl.ds(8 + row, NX, stride=YPAD), :]
            rows[pl.ds(n * 32, NX), :] = edge
            ys[p, n // 2, n % 2] = hat_lanes(edge)
            raw = field[pl.ds(2 * NY + row, NX, stride=NY), :]
            up, down = across(raw[NX - 8:], 0, 8, 1, 1), across(raw[:8], 0, 8, 1, -1)
            corner[pl.ds(n * 32, 8), :] = up
            corner[pl.ds(n * 32 + NX - 8, 8), :] = down
            store_pair(xys.at[p, 1, n // 2, pl.ds(2 * (n % 2), 2)], hat_lanes(up), 0)
            store_pair(xys.at[p, 0, n // 2, pl.ds(2 * (n % 2), 2)], hat_lanes(down), 6)
        turned = rows[...].T
        for sz, part_z in enumerate((turned[0:8], turned[120:128])):
            for sy in range(2):
                store_pair(yzs.at[p, sy, sz], across(part_z, 1, 128, 32, 2 * sy - 1), 6 * sz)
        turned = corner[...].T
        lane = lax.rem(iota((8, 128), 1), 32)
        for sz, part_z in enumerate((turned[0:8], turned[120:128])):
            for sy in range(2):
                both = across(part_z, 1, 128, 32, 2 * sy - 1)
                store_pair(xyzs.at[p, 1, sy, sz], jnp.where(lane < 8, both, 0.0), 6 * sz)
                store_pair(xyzs.at[p, 0, sy, sz], jnp.where(lane < 8, 0.0, both), 6 * sz)

        for k in range(GROUPS):
            v = jnp.concatenate([hat_rows(g, (4 * k + n) * YPAD) for n in range(4)], 0)
            ref[pl.ds(k * 128, 128), :] = hat_lanes(v)
            turned = v.T
            store_pair(zs.at[p, 0, pl.ds(2 * k, 2)], turned[0:8], 0)
            store_pair(zs.at[p, 1, pl.ds(2 * k, 2)], turned[120:128], 6)

    def send_filter(p, along_y, when=None, faces=(True, False)):
        for d in DIRECTIONS:
            if d[1] == along_y and (d == (0, along_y, 0)) in faces:
                go = inside(d) if when is None else jnp.logical_and(inside(d), when)

                @pl.when(go)
                def _(d=d):
                    filter_copy(p, d).start()

    def send_lower(along_y, when=None):
        for d in sorted(LOWER, key=lambda d: (d[0] != 0 if along_y == 0 else 0, -sum(map(abs, d)))):
            if d[1] == along_y:
                go = inside(d) if when is None else jnp.logical_and(inside(d), when)

                @pl.when(go)
                def _(d=d):
                    lower_copy(d).start()

    up_far, down_far = my_core == 1, my_core == 0

    def wait_received(p, along_y):
        for d in reversed(DIRECTIONS):
            if bool(d[1]) == along_y:
                @pl.when(inside(tuple(-s for s in d)))
                def _(d=d):
                    filter_copy(p, d).wait_recv()

    def add_xz(p, acc):
        wait_received(p, False)
        def add(layer, v):
            acc[pl.ds(layer * NY, NY), :] = acc[pl.ds(layer * NY, NY), :] + v

        first, second = xr[p, 1, pl.ds(0, NY), :], xr[p, 1, pl.ds(NY, NY), :]
        add(0, first + 2.0 * second)
        add(1, second)
        first, second = xr[p, 0, pl.ds(0, NY), :], xr[p, 0, pl.ds(NY, NY), :]
        add(NX - 2, first)
        add(NX - 1, 2.0 * first + second)
        for k in range(GROUPS):
            low, high = [[zr[p, sz, 2 * k + i] for i in range(2)] for sz in (1, 0)]
            edge = {0: 1, GROUPS - 1: 0}.get(k)
            if edge is not None:
                low, high = [[v[i] + xzr[p, edge, sz, i] for i in range(2)] for v, sz in ((low, 1), (high, 0))]
            acc[pl.ds(k * 128, 128), :] = acc[pl.ds(k * 128, 128), :] + z_edges(low, high)

    def add_y(p, acc):
        wait_received(p, True)
        low, high = [[sum([yzr[p, sy, sz, i] for sy in range(2)] + [
            xyzr[p, sx, sy, sz, i] for sx in range(2) for sy in range(2)]) for i in range(2)] for sz in (1, 0)]
        turned = z_edges(low, high)
        at = {}
        for sy in range(2):
            for n in range(2):
                center = yr[p, sy, n]
                up, down = [[xyr[p, sx, sy, 2 * n + i] for i in range(2)] for sx in (1, 0)]
                at[sy, n] = jnp.concatenate([
                    center[:8] + rows_at({0: up[0], 1: up[1]}), center[8:16],
                    center[16:] + rows_at({6: down[0], 7: down[1]})], 0)
        for n, (row, v) in enumerate((
                (0, at[1, 0] + 2.0 * at[1, 1]), (1, at[1, 1]), (NY - 2, at[0, 0]), (NY - 1, 2.0 * at[0, 0] + at[0, 1]))):
            place = pl.ds(row, NX, stride=NY)
            acc[place, :] = acc[place, :] + v + turned[n * 32:n * 32 + NX]

    load_density.wait()
    local_filter(0, acc)
    load_nodes.wait()

    def first_columns(v):
        lane = iota(v[0].shape, 1)
        return jnp.where(lane == 0, v[0], jnp.where(
            lane == 1, pltpu.roll(v[1], 1, 1), jnp.where(lane == 2, pltpu.roll(v[2], 2, 1), 0.0)))

    for m in range(3):
        dys[m] = nodes[m, pl.ds(0, NX, stride=NY), :]
        dxys[m] = dys[m, pl.ds(0, 1), :]
    for k in range(GROUPS):
        columns = first_columns([nodes[m, pl.ds(k * 128, 128), :] for m in range(3)])
        turned = columns.T[0:8]
        for m in range(3):
            dzs[3 * k + m] = turned[m:m + 1]
        if k == 0:
            m6[pl.ds(0, NY), :] = columns[:NY]
    m6[pl.ds(NY, NX), :] = first_columns([dys[m] for m in range(3)])
    turned = m6[...].T[0:8]
    lane8 = iota((8, 128), 1)
    for target, tile in (
            (dxzs, jnp.where(lane8 < NY, turned, 0.0)),
            (dyzs, jnp.where(jnp.logical_and(lane8 >= NY, lane8 < NY + NX), turned, 0.0)),
            (dxyzs, jnp.where(lane8 == NY + NX, pltpu.roll(turned, NY + NX, 1), 0.0))):
        for m in range(3):
            target[m] = tile[m:m + 1]

    pl.semaphore_wait(barrier, waits)
    send_filter(0, 1, up_far, (False,))
    send_lower(-1, down_far)
    send_filter(0, -1, down_far)
    send_lower(0)
    send_filter(0, 1, up_far, (True,))
    send_filter(0, 0)
    send_lower(-1, up_far)
    send_filter(0, -1, up_far)
    send_filter(0, 1, down_far)

    def wait_lower(*directions):
        for d in LOWER:
            if d in directions:
                @pl.when(inside(tuple(-s for s in d)))
                def _(d=d):
                    lower_copy(d).wait_recv()

    rest = jnp.zeros((120, 128), F32)

    def z_pass(base, count, packed):
        halo = jnp.concatenate([rows_at(dict(enumerate(packed))), rest], 0).T[:count]
        lane = iota(halo.shape, 1)
        out = []
        for m in range(3):
            u = nodes[m, pl.ds(base, count), :]
            up = jnp.where(lane == NZ - 1, pltpu.roll(halo, NZ - 1 - m, 1), pltpu.roll(u, NZ - 1, 1))
            out += [u + up, up - u]
        return out

    wait_lower((0, 0, -1))
    for k in range(GROUPS):
        for n, v in enumerate(z_pass(k * 128, 128, [dzr[3 * k + m] for m in range(3)])):
            for i in range(4):
                sd[n, pl.ds((4 * k + i) * NODE_PAD, NY), :] = v[i * NY:(i + 1) * NY]

    def yz_terms(i, t):
        base = pl.multiple_of(i * NODE_PAD, 8) + 8 * t
        out = []
        for k in range(6):
            here, above = sd[k, pl.ds(base, 8), :], sd[k, pl.ds(base + 1, 8), :]
            out += [here + above, above - here]
        return out

    square = lambda v: v * v

    def energies(t, first, end):
        def element(i, before):
            now = yz_terms(i, t)
            w = []
            for m in range(3):
                (a0, a1, a2, a3), (b0, b1, b2, b3) = now[4 * m:4 * m + 4], before[4 * m:4 * m + 4]
                w.append({100: a0 - b0, 110: a1 - b1, 101: a2 - b2, 111: a3 - b3,
                          10: a1 + b1, 1: a2 + b2, 11: a3 + b3})
            u, v, z = w
            total = (LAME / 16) * square(u[100] + v[10] + z[1])
            total += (LAME / 48) * (square(v[110] + z[101]) + square(u[110] + z[11]) + square(u[101] + v[11]))
            total += (SHEAR / 8) * (square(u[100]) + square(v[10]) + square(z[1]))
            total += (SHEAR / 16) * (
                (square(u[110]) + square(u[101]) + square(v[110])) + (square(v[11]) + square(z[101]) + square(z[11]))
                + (square(u[10] + v[100]) + square(v[1] + z[10]) + square(u[1] + z[100])))
            total += (SHEAR / 48) * (square(u[11] + v[101]) + square(v[101] + z[110]) + square(u[11] + z[110]))
            total += ((LAME + 4 * SHEAR) / 144) * (square(u[111]) + square(v[111]) + square(z[111]))
            energy[pl.ds(pl.multiple_of((i - 1) * NY, NY) + 8 * t, 8), :] = total
            return now

        def pair(n, before):
            return tuple(element(2 * n + 2, element(2 * n + 1, before)))

        lax.fori_loop(first, end, pair, tuple(yz_terms(2 * first, t)))

    for t in range(NY // 8 - 1):
        energies(t, 0, NX // 2 - 1)
    wait_lower((-1, 0, 0), (-1, 0, -1))
    for n, v in enumerate(z_pass(ROWS, NY, [dxzr[m] for m in range(3)])):
        sd[n, pl.ds(NX * NODE_PAD, NY), :] = v
    for t in range(NY // 8 - 1):
        energies(t, NX // 2 - 1, NX // 2)
    add_xz(0, acc)
    wait_lower(*[d for d in LOWER if d[1]])
    for m in range(3):
        nodes[m, pl.ds(ROWS + NY + NX, 1), :] = dxyr[m]
    for n, v in enumerate(z_pass(ROWS + NY, NY, [pltpu.roll(dyzr[m] + dxyzr[m], 128 - NY, 1) for m in range(3)])):
        sd[n, pl.ds(NY, NX + 1, stride=NODE_PAD), :] = v[:NX + 1]
    energies(NY // 8 - 1, 0, NX // 2)

    def inverse_cover(index, extent):
        end = extent - 1
        return jnp.where(jnp.logical_or(index == 0, index == end), 1.0 / 6.0, jnp.where(
            jnp.logical_or(index == 1, index == end - 1), 1.0 / 8.0, 1.0 / 9.0)).astype(F32)

    inverse_yz = inverse_cover(iota((NY, NZ), 0) + gy * NY, NY * size_y) * inverse_cover(
        iota((NY, NZ), 1) + gz * NZ, NZ * size_z)

    def weigh(physical, energies_, inverse):
        product = physical * physical * energies_
        return -3.0 * product * inverse, physical * product

    y_rows = (0, 1, NY - 2, NY - 1)
    total = jnp.zeros((NY, NZ), F32)
    for i in range(NX):
        inverse = inverse_yz * inverse_cover(gx * NX + i, NX * size_x)
        slope, term = weigh(acc[pl.ds(i * NY, NY), :] * inverse, energy[pl.ds(i * NY, NY), :], inverse)
        field[pl.ds((i + 2) * NY, NY), :] = slope
        total = total + term
    row = iota((NY, NZ), 0)
    inner = jnp.logical_and(row >= 2, row < NY - 2)
    total = jnp.sum(jnp.where(inner, total, 0.0), axis=0, keepdims=True)

    inverse_x = inverse_cover(iota((NX, NZ), 0) + gx * NX, NX * size_x)
    inverses = [inverse_x * inverse_yz[row:row + 1] for row in y_rows]
    energy_rows = [energy[pl.ds(row, NX, stride=NY), :] for row in y_rows]
    add_y(0, acc)
    rows_total = jnp.zeros((NX, NZ), F32)
    for n, row in enumerate(y_rows):
        slope, term = weigh(acc[pl.ds(row, NX, stride=NY), :] * inverses[n], energy_rows[n], inverses[n])
        field[pl.ds(2 * NY + row, NX, stride=NY), :] = slope
        rows_total = rows_total + term
    total = total + jnp.sum(rows_total, axis=0, keepdims=True)

    def sum_copy(s, mine, to):
        return remote(part.at[s], part_in.at[s, mine], psend_sem.at[s], precv_sem.at[s], to)

    def sum_wait(sem, s, n):
        whole = part_in.at[s, pl.ds(0, n)]
        pltpu.make_async_copy(whole, whole, sem.at[s]).wait()

    mine = my_z * 2 + my_core
    part[0] = total
    for z, c in column:
        @pl.when(other(z, c))
        def _(z=z, c=c):
            sum_copy(0, mine, at_zc(z, c)).start()
    local_filter(1, out)
    for along_y in (1, 0, -1):
        send_filter(1, along_y)

    @pl.when(early)
    def _():
        part_in[0, mine] = total
        sum_wait(precv_sem, 0, 2 * count_z - 1)
        partial = jnp.sum(part_in[0, 0:2 * count_z], axis=0)
        here = gz * ring_y + my_y
        part[1] = partial
        part_in[1, here] = partial
        for o in plane:
            sum_copy(1, here, partner_xy(*o)).start()

    add_xz(1, out)
    add_y(1, out)

    for d in DIRECTIONS:
        @pl.when(inside(d))
        def _(d=d):
            for p in range(2):
                filter_copy(p, d).wait_send()
            if d in lower:
                lower_copy(d).wait_send()

    @pl.when(early)
    def _():
        sum_wait(psend_sem, 0, 2 * layers_z - 1)
        sum_wait(psend_sem, 1, len(plane))
        sum_wait(precv_sem, 1, len(plane))
        part[2] = jnp.sum(part_in[1, 0:len(plane) + 1], axis=0)

    def pass_on(z, c):
        return remote(
            part.at[2], part_in.at[2, 0], pass_sem.at[2 * (z - layers_z) + c], precv_sem.at[2], at_zc(z, c))

    for z, c in serves:
        @pl.when(serving(z))
        def _(z=z, c=c):
            pass_on(z, c).start()

    @pl.when(jnp.logical_not(early))
    def _():
        sum_wait(psend_sem, 0, 2 * layers_z)
        if halves > 1:
            sum_wait(precv_sem, 2, 1)
            part[2] = part_in[2, 0]

    total_out[...] = jnp.broadcast_to(jnp.sum(part[2], axis=1, keepdims=True), (8, 128))

    for z, c in serves:
        @pl.when(serving(z))
        def _(z=z, c=c):
            pass_on(z, c).wait_send()


def exchange(mesh, density, displacement):
    sizes = (mesh.shape["gx"], mesh.shape["gy"], mesh.shape["gz"], min(8, mesh.shape["gx"]))
    vmem = lambda *shape: pltpu.VMEM(shape, F32)
    partners = max(sizes[0] // sizes[3] * sizes[1], sizes[3] * sizes[2])
    scratch = [
        vmem((NX + 4) * NY, NZ), vmem(NX * YPAD, NZ), vmem(4 * YPAD, NZ), vmem(ROWS, NZ),
        vmem(128, NZ), vmem(128, NZ), vmem(3, ROWS + 2 * NY, NZ),
        vmem(6, 32 * NODE_PAD, NZ), vmem(ROWS, NZ)]
    filters = [vmem(2, 2, 2 * NY, NZ), vmem(2, 2, 2, NX, NZ), vmem(3, 2, 2, 4, 1, NZ), vmem(3, 2, 2 * GROUPS, 1, 128),
               vmem(3, 2, 2, 2, 1, 128), vmem(3, 2, 2, 2, 1, 128), vmem(3, 2, 2, 2, 2, 1, 128)]
    scratch += filters + filters
    edges = [vmem(11, 1, NZ), vmem(3 * GROUPS + 8, 1, 128), vmem(11, 1, 128), vmem(11, 1, 128), vmem(11, 1, 128)]
    scratch += [vmem(3, NX, NZ)] + edges + edges + [vmem(128, 128)]
    scratch += [vmem(11, 1, 128), vmem(4, partners, 1, 128)]
    dma = pltpu.SemaphoreType.DMA
    scratch += [dma((2, 27)), dma((2, 27)), dma((8,)), dma((8,)), dma((2,)), dma((3,)), dma((3,)), dma((8,))]
    return pl.pallas_call(
        functools.partial(kernel, sizes),
        out_shape=[jax.ShapeDtypeStruct((ROWS, NZ), F32), jax.ShapeDtypeStruct((8, 128), F32)],
        in_specs=[pl.BlockSpec(memory_space=pltpu.HBM)] * 2,
        out_specs=[pl.BlockSpec(memory_space=pltpu.VMEM)] * 2,
        scratch_shapes=scratch,
        compiler_params=pltpu.CompilerParams(
            collective_id=0, has_side_effects=True, vmem_limit_bytes=56_000_000),
        cost_estimate=pl.CostEstimate(flops=20_000_000, bytes_accessed=2_000_000, transcendentals=0),
    )(density, displacement)


def scale_kernel(elements, field, total, out, mean_out, scaled, mean_ref, sem):
    mean = total[0:1, :] / elements
    mean_ref[...] = mean[:, 0:1]
    inverse = 1.0 / mean
    copies = [pltpu.make_async_copy(mean_ref, mean_out, sem.at[PARTS])]
    copies[0].start()
    for n in range(PARTS):
        part = pl.ds(n * (ROWS // PARTS), ROWS // PARTS)
        scaled[part, :] = field[part, :] * inverse
        copies.append(pltpu.make_async_copy(scaled.at[part], out.at[part], sem.at[n]))
        copies[-1].start()
    for copy in copies:
        copy.wait()


def solution(mesh):
    def shards(displacement, density):
        filtered, total = exchange(mesh, density.reshape(ROWS, NZ), displacement.reshape(3, ROWS, NZ))
        sensitivity, mean = pl.pallas_call(
            functools.partial(scale_kernel, float(ROWS * NZ * mesh.size)),
            out_shape=[jax.ShapeDtypeStruct((ROWS, NZ), F32), jax.ShapeDtypeStruct((1, 1), F32)],
            in_specs=[pl.BlockSpec(memory_space=pltpu.VMEM)] * 2,
            out_specs=[pl.BlockSpec(memory_space=pl.ANY)] * 2,
            scratch_shapes=[
                pltpu.VMEM((ROWS, NZ), F32), pltpu.VMEM((1, 1), F32), pltpu.SemaphoreType.DMA((PARTS + 1,))],
            compiler_params=pltpu.CompilerParams(vmem_limit_bytes=4 * 2**20),
        )(filtered, total)
        return sensitivity.reshape(NX, NY, NZ), mean.reshape(())

    return jax.shard_map(
        shards,
        mesh=mesh,
        in_specs=(P(None, "gx", "gy", "gz"), P("gx", "gy", "gz")),
        out_specs=(P("gx", "gy", "gz"), P()),
        check_vma=False,
    )
```

```python
import functools
import itertools

import jax
import jax.numpy as jnp
from jax import lax
from jax.experimental import pallas as pl
from jax.experimental.pallas import tpu as pltpu
from jax.sharding import PartitionSpec as P

MESH = pl.DeviceIdType.MESH
F32 = jnp.float32
NX, NY, NZ = 24, 32, 128
ROWS = NX * NY
GROUPS = ROWS // 128
YPAD = 48
NODE_PAD = 40
PARTS = 4
LAME = 0.3 / (1.3 * 0.4)
SHEAR = 1.0 / 2.6

DIRECTIONS = sorted((d for d in itertools.product((-1, 0, 1), repeat=3) if any(d)), key=lambda d: (not d[1], -sum(map(abs, d))))
LOWER = [d for d in DIRECTIONS if max(d) <= 0]


def slot(direction):
    return (direction[0] + 1) * 9 + (direction[1] + 1) * 3 + direction[2] + 1


def lower_slot(direction):
    return -(direction[0] * 4 + direction[1] * 2 + direction[2])


def iota(shape, axis):
    return lax.broadcasted_iota(jnp.int32, shape, axis)


def hat_lanes(v):
    lane = iota(v.shape, v.ndim - 1)
    axis = v.ndim - 1

    def moved(step):
        rolled = pltpu.roll(v, step % NZ, axis)
        return jnp.where(lane >= step if step > 0 else lane < NZ + step, rolled, 0.0)

    return 3.0 * v + 2.0 * (moved(1) + moved(-1)) + (moved(2) + moved(-2))


def across(v, axis, size, step, direction):
    place = iota(v.shape, axis) // step
    count = size // step
    if direction > 0:
        two, one = pltpu.roll(v, 2 * step, axis), pltpu.roll(v, step, axis)
        return jnp.where(place == 0, two + 2.0 * one, jnp.where(place == 1, two, 0.0))
    two, one = pltpu.roll(v, size - 2 * step, axis), pltpu.roll(v, size - step, axis)
    return jnp.where(place == count - 1, two + 2.0 * one, jnp.where(place == count - 2, two, 0.0))


def rows_at(places):
    row = iota((8, NZ), 0)
    tile = jnp.zeros((8, NZ), F32)
    for place, value in places.items():
        tile = jnp.where(row == place, jnp.broadcast_to(value, (8, NZ)), tile)
    return tile


def kernel(sizes, density, displacement, out, total_out, *scratch):
    (field, g, b4, acc, rows, corner, nodes, sd, energy,
     xs, ys, xys, zs, xzs, yzs, xyzs, xr, yr, xyr, zr, xzr, yzr, xyzr,
     dys, dxys, dzs, dxzs, dyzs, dxyzs, dxyr, dzr, dxzr, dyzr, dxyzr, m6,
     part, part_in, send_sem, recv_sem, dsend_sem, drecv_sem, load_sem, psend_sem, precv_sem, pass_sem) = scratch
    size_x, size_y, size_z, ring_y = sizes
    gx, gy, gz = (lax.axis_index(a) for a in ("gx", "gy", "gz"))

    def inside(direction):
        ok = []
        for place, step, count in zip((gx, gy, gz), direction, (size_x, size_y, size_z)):
            if step > 0:
                ok.append(place < count - 1)
            elif step < 0:
                ok.append(place > 0)
        return functools.reduce(jnp.logical_and, ok)

    def device(direction):
        return (gx + direction[0], gy + direction[1], gz + direction[2])

    layers_z = size_x // ring_y
    my_y, my_z = lax.rem(gx, ring_y), gx // ring_y + layers_z * (gy // 2)
    my_core = lax.rem(gy, 2)
    count_z = layers_z * (size_y // 2)

    halves = size_y // 2
    early = gy < 2

    def at_zc(z, c):
        return (lax.rem(z, layers_z) * ring_y + my_y, (z // layers_z) * 2 + c, gz)

    def partner_xy(dx, dy):
        x, y = lax.rem(gz + dx, size_z), lax.rem(my_y + dy, ring_y)
        return ((gx // ring_y) * ring_y + y, gy, x)

    server = layers_z - 1 - (my_z - layers_z) // 2
    serves = [(z, c) for z in range(layers_z, count_z) for c in range(2)]

    def serving(z):
        return jnp.logical_and(my_z == layers_z - 1 - (z - layers_z) // 2, my_core == 1)

    column = [(z, c) for z in range(layers_z) for c in range(2)]

    def other(z, c):
        return jnp.logical_or(my_z != z, my_core != c)

    def far_first(counts):
        offs = [o for o in itertools.product(*[range(c) for c in counts]) if any(o)]
        return sorted(offs, key=lambda o: -sum(min(s, c - s) for s, c in zip(o, counts)))

    plane = far_first((size_z, ring_y))

    load_density = pltpu.make_async_copy(density, field.at[pl.ds(2 * NY, ROWS)], load_sem.at[0])
    load_nodes = pltpu.make_async_copy(displacement, nodes.at[:, pl.ds(0, ROWS)], load_sem.at[1])
    load_density.start()
    load_nodes.start()

    barrier = pltpu.get_barrier_semaphore()

    def greet(to):
        pl.semaphore_signal(barrier, inc=1, device_id=to, device_id_type=MESH)

    waits = 0
    for d in DIRECTIONS:
        @pl.when(inside(d))
        def _(d=d):
            greet(device(d))
        waits = waits + inside(d).astype(jnp.int32)

    @pl.when(early)
    def _():
        for z, c in [(z, c) for z in range(count_z) for c in range(2)]:
            @pl.when(other(z, c))
            def _(z=z, c=c):
                greet(at_zc(z, c))
        for o in plane:
            greet(partner_xy(*o))

    if halves > 1:
        @pl.when(jnp.logical_not(early))
        def _():
            greet(at_zc(server, 1))

    served = sum(serving(z).astype(jnp.int32) for z, _ in serves) if serves else 0
    waits = waits + jnp.where(early, 2 * layers_z - 1 + len(plane) + served, 2 * layers_z)

    zero_row = jnp.zeros((8, NZ), F32)

    def zero(ref):
        ref[...] = jnp.zeros(ref.shape, F32)

    received = {}
    for d in DIRECTIONS:
        sx, sy, sz = ((s + 1) // 2 for s in d)
        kind = tuple(bool(s) for s in d)
        received[d] = {
            (True, False, False): lambda p: (xs.at[p, sx], xr.at[p, sx]),
            (False, True, False): lambda p: (ys.at[p, sy], yr.at[p, sy]),
            (True, True, False): lambda p: (xys.at[p, sx, sy], xyr.at[p, sx, sy]),
            (False, False, True): lambda p: (zs.at[p, sz], zr.at[p, sz]),
            (True, False, True): lambda p: (xzs.at[p, sx, sz], xzr.at[p, sx, sz]),
            (False, True, True): lambda p: (yzs.at[p, sy, sz], yzr.at[p, sy, sz]),
            (True, True, True): lambda p: (xyzs.at[p, sx, sy, sz], xyzr.at[p, sx, sy, sz]),
        }[kind]
        received[d] = [received[d](p) for p in range(2)]
    lower = {
        (-1, 0, 0): (nodes.at[:, pl.ds(0, NY)], nodes.at[:, pl.ds(ROWS, NY)]),
        (0, -1, 0): (dys, nodes.at[:, pl.ds(ROWS + NY, NX)]),
        (-1, -1, 0): (dxys.at[pl.ds(0, 3)], dxyr.at[pl.ds(0, 3)]),
        (0, 0, -1): (dzs.at[pl.ds(0, 3 * GROUPS)], dzr.at[pl.ds(0, 3 * GROUPS)]),
        (-1, 0, -1): (dxzs.at[pl.ds(0, 3)], dxzr.at[pl.ds(0, 3)]),
        (0, -1, -1): (dyzs.at[pl.ds(0, 3)], dyzr.at[pl.ds(0, 3)]),
        (-1, -1, -1): (dxyzs.at[pl.ds(0, 3)], dxyzr.at[pl.ds(0, 3)]),
    }

    for d in DIRECTIONS:
        @pl.when(jnp.logical_not(inside(tuple(-s for s in d))))
        def _(d=d):
            for p in range(2):
                zero(received[d][p][1])
            if d in lower:
                zero(lower[d][1])

    def remote(source, target, send, recv, to):
        return pltpu.make_async_remote_copy(
            src_ref=source, dst_ref=target, send_sem=send, recv_sem=recv, device_id=to, device_id_type=MESH)

    def filter_copy(p, d):
        source, target = received[d][p]
        return remote(source, target, send_sem.at[p, slot(d)], recv_sem.at[p, slot(d)], device(d))

    def lower_copy(d):
        source, target = lower[d]
        return remote(source, target, dsend_sem.at[lower_slot(d)], drecv_sem.at[lower_slot(d)], device(d))

    for margin in (0, NY, (NX + 2) * NY, (NX + 3) * NY):
        field[pl.ds(margin, NY), :] = jnp.zeros((NY, NZ), F32)

    for i in range(NX):
        g[pl.ds(i * YPAD, 8), :] = zero_row
        g[pl.ds(i * YPAD + 40, 8), :] = zero_row
    for i in range(4):
        b4[pl.ds(i * YPAD, 8), :] = zero_row
        b4[pl.ds(i * YPAD + 40, 8), :] = zero_row
    zero(rows)
    zero(corner)
    zero(m6)

    middle = jnp.zeros((112, 128), F32)

    def hat_rows(ref, base):
        at = [ref[pl.ds(base + 6 + k, NY), :] for k in range(5)]
        return 3.0 * at[2] + 2.0 * (at[1] + at[3]) + (at[0] + at[4])

    def store_pair(ref, tile, first):
        ref[0] = tile[first:first + 1]
        ref[1] = tile[first + 1:first + 2]

    def z_edges(low, high):
        return jnp.concatenate([
            rows_at({0: low[0] + 2.0 * low[1], 1: low[1]}), middle,
            rows_at({6: high[0], 7: 2.0 * high[0] + high[1]})], 0).T

    def local_filter(p, ref):
        for n, layer in enumerate((0, 1, NX - 2, NX - 1)):
            b4[pl.ds(n * YPAD + 8, NY), :] = field[pl.ds((layer + 2) * NY, NY), :]
        faces = [hat_rows(b4, n * YPAD) for n in range(4)]
        for n in range(4):
            xs[p, n // 2, pl.ds((n % 2) * NY, NY), :] = hat_lanes(faces[n])
        turned = jnp.concatenate(faces, 0).T
        for sz, part_z in enumerate((turned[0:8], turned[120:128])):
            for sx in range(2):
                store_pair(xzs.at[p, sx, sz], across(part_z, 1, 128, 32, 2 * sx - 1), 6 * sz)

        for t in range(NY // 8):
            at = [field[pl.ds(i * NY + 8 * t, 8), :] for i in range(NX + 4)]
            for i in range(NX):
                g[pl.ds(i * YPAD + 8 + 8 * t, 8), :] = (
                    3.0 * at[i + 2] + 2.0 * (at[i + 1] + at[i + 3]) + (at[i] + at[i + 4]))

        for n, row in enumerate((0, 1, NY - 2, NY - 1)):
            edge = g[pl.ds(8 + row, NX, stride=YPAD), :]
            rows[pl.ds(n * 32, NX), :] = edge
            ys[p, n // 2, n % 2] = hat_lanes(edge)
            raw = field[pl.ds(2 * NY + row, NX, stride=NY), :]
            up, down = across(raw[NX - 8:], 0, 8, 1, 1), across(raw[:8], 0, 8, 1, -1)
            corner[pl.ds(n * 32, 8), :] = up
            corner[pl.ds(n * 32 + NX - 8, 8), :] = down
            store_pair(xys.at[p, 1, n // 2, pl.ds(2 * (n % 2), 2)], hat_lanes(up), 0)
            store_pair(xys.at[p, 0, n // 2, pl.ds(2 * (n % 2), 2)], hat_lanes(down), 6)
        turned = rows[...].T
        for sz, part_z in enumerate((turned[0:8], turned[120:128])):
            for sy in range(2):
                store_pair(yzs.at[p, sy, sz], across(part_z, 1, 128, 32, 2 * sy - 1), 6 * sz)
        turned = corner[...].T
        lane = lax.rem(iota((8, 128), 1), 32)
        for sz, part_z in enumerate((turned[0:8], turned[120:128])):
            for sy in range(2):
                both = across(part_z, 1, 128, 32, 2 * sy - 1)
                store_pair(xyzs.at[p, 1, sy, sz], jnp.where(lane < 8, both, 0.0), 6 * sz)
                store_pair(xyzs.at[p, 0, sy, sz], jnp.where(lane < 8, 0.0, both), 6 * sz)

        for k in range(GROUPS):
            v = jnp.concatenate([hat_rows(g, (4 * k + n) * YPAD) for n in range(4)], 0)
            ref[pl.ds(k * 128, 128), :] = hat_lanes(v)
            turned = v.T
            store_pair(zs.at[p, 0, pl.ds(2 * k, 2)], turned[0:8], 0)
            store_pair(zs.at[p, 1, pl.ds(2 * k, 2)], turned[120:128], 6)

    def send_filter(p, along_y, when=None, faces=(True, False)):
        for d in DIRECTIONS:
            if d[1] == along_y and (d == (0, along_y, 0)) in faces:
                go = inside(d) if when is None else jnp.logical_and(inside(d), when)

                @pl.when(go)
                def _(d=d):
                    filter_copy(p, d).start()

    def send_lower(along_y, when=None):
        for d in sorted(LOWER, key=lambda d: (d[0] != 0 if along_y == 0 else 0, -sum(map(abs, d)))):
            if d[1] == along_y:
                go = inside(d) if when is None else jnp.logical_and(inside(d), when)

                @pl.when(go)
                def _(d=d):
                    lower_copy(d).start()

    up_far, down_far = my_core == 1, my_core == 0

    def wait_received(p, along_y, along_z=(False, True)):
        for d in reversed(DIRECTIONS):
            if bool(d[1]) == along_y and bool(d[2]) in along_z:
                @pl.when(inside(tuple(-s for s in d)))
                def _(d=d):
                    filter_copy(p, d).wait_recv()

    def add_xz(p, acc):
        wait_received(p, False)
        def add(layer, v):
            acc[pl.ds(layer * NY, NY), :] = acc[pl.ds(layer * NY, NY), :] + v

        first, second = xr[p, 1, pl.ds(0, NY), :], xr[p, 1, pl.ds(NY, NY), :]
        add(0, first + 2.0 * second)
        add(1, second)
        first, second = xr[p, 0, pl.ds(0, NY), :], xr[p, 0, pl.ds(NY, NY), :]
        add(NX - 2, first)
        add(NX - 1, 2.0 * first + second)
        for k in range(GROUPS):
            low, high = [[zr[p, sz, 2 * k + i] for i in range(2)] for sz in (1, 0)]
            edge = {0: 1, GROUPS - 1: 0}.get(k)
            if edge is not None:
                low, high = [[v[i] + xzr[p, edge, sz, i] for i in range(2)] for v, sz in ((low, 1), (high, 0))]
            acc[pl.ds(k * 128, 128), :] = acc[pl.ds(k * 128, 128), :] + z_edges(low, high)

    def add_y(p, acc):
        wait_received(p, True, (False,))
        at = {}
        for sy in range(2):
            for n in range(2):
                center = yr[p, sy, n]
                up, down = [[xyr[p, sx, sy, 2 * n + i] for i in range(2)] for sx in (1, 0)]
                at[sy, n] = jnp.concatenate([
                    center[:8] + rows_at({0: up[0], 1: up[1]}), center[8:16],
                    center[16:] + rows_at({6: down[0], 7: down[1]})], 0)
        for n, (row, v) in enumerate((
                (0, at[1, 0] + 2.0 * at[1, 1]), (1, at[1, 1]), (NY - 2, at[0, 0]), (NY - 1, 2.0 * at[0, 0] + at[0, 1]))):
            place = pl.ds(row, NX, stride=NY)
            acc[place, :] = acc[place, :] + v
        wait_received(p, True, (True,))
        low, high = [[sum([yzr[p, sy, sz, i] for sy in range(2)] + [
            xyzr[p, sx, sy, sz, i] for sx in range(2) for sy in range(2)]) for i in range(2)] for sz in (1, 0)]
        turned = z_edges(low, high)
        for n, row in enumerate((0, 1, NY - 2, NY - 1)):
            place = pl.ds(row, NX, stride=NY)
            acc[place, :] = acc[place, :] + turned[n * 32:n * 32 + NX]

    load_density.wait()
    local_filter(0, acc)
    load_nodes.wait()

    def first_columns(v):
        lane = iota(v[0].shape, 1)
        return jnp.where(lane == 0, v[0], jnp.where(
            lane == 1, pltpu.roll(v[1], 1, 1), jnp.where(lane == 2, pltpu.roll(v[2], 2, 1), 0.0)))

    for m in range(3):
        dys[m] = nodes[m, pl.ds(0, NX, stride=NY), :]
        dxys[m] = dys[m, pl.ds(0, 1), :]
    for k in range(GROUPS):
        columns = first_columns([nodes[m, pl.ds(k * 128, 128), :] for m in range(3)])
        turned = columns.T[0:8]
        for m in range(3):
            dzs[3 * k + m] = turned[m:m + 1]
        if k == 0:
            m6[pl.ds(0, NY), :] = columns[:NY]
    m6[pl.ds(NY, NX), :] = first_columns([dys[m] for m in range(3)])
    turned = m6[...].T[0:8]
    lane8 = iota((8, 128), 1)
    for target, tile in (
            (dxzs, jnp.where(lane8 < NY, turned, 0.0)),
            (dyzs, jnp.where(jnp.logical_and(lane8 >= NY, lane8 < NY + NX), turned, 0.0)),
            (dxyzs, jnp.where(lane8 == NY + NX, pltpu.roll(turned, NY + NX, 1), 0.0))):
        for m in range(3):
            target[m] = tile[m:m + 1]

    pl.semaphore_wait(barrier, waits)
    send_filter(0, 1, up_far, (False,))
    send_lower(-1, down_far)
    send_filter(0, -1, down_far)
    send_lower(0)
    send_filter(0, 1, up_far, (True,))
    send_filter(0, 0)
    send_lower(-1, up_far)
    send_filter(0, -1, up_far)
    send_filter(0, 1, down_far)

    def wait_lower(*directions):
        for d in LOWER:
            if d in directions:
                @pl.when(inside(tuple(-s for s in d)))
                def _(d=d):
                    lower_copy(d).wait_recv()

    rest = jnp.zeros((120, 128), F32)

    def z_pass(base, count, packed):
        halo = jnp.concatenate([rows_at(dict(enumerate(packed))), rest], 0).T[:count]
        lane = iota(halo.shape, 1)
        out = []
        for m in range(3):
            u = nodes[m, pl.ds(base, count), :]
            up = jnp.where(lane == NZ - 1, pltpu.roll(halo, NZ - 1 - m, 1), pltpu.roll(u, NZ - 1, 1))
            out += [u + up, up - u]
        return out

    wait_lower((0, 0, -1))
    for k in range(GROUPS):
        for n, v in enumerate(z_pass(k * 128, 128, [dzr[3 * k + m] for m in range(3)])):
            for i in range(4):
                sd[n, pl.ds((4 * k + i) * NODE_PAD, NY), :] = v[i * NY:(i + 1) * NY]

    def yz_terms(i, t):
        base = pl.multiple_of(i * NODE_PAD, 8) + 8 * t
        out = []
        for k in range(6):
            here, above = sd[k, pl.ds(base, 8), :], sd[k, pl.ds(base + 1, 8), :]
            out += [here + above, above - here]
        return out

    square = lambda v: v * v

    def energies(t, first, end):
        def element(i, before):
            now = yz_terms(i, t)
            w = []
            for m in range(3):
                (a0, a1, a2, a3), (b0, b1, b2, b3) = now[4 * m:4 * m + 4], before[4 * m:4 * m + 4]
                w.append({100: a0 - b0, 110: a1 - b1, 101: a2 - b2, 111: a3 - b3,
                          10: a1 + b1, 1: a2 + b2, 11: a3 + b3})
            u, v, z = w
            total = (LAME / 16) * square(u[100] + v[10] + z[1])
            total += (LAME / 48) * (square(v[110] + z[101]) + square(u[110] + z[11]) + square(u[101] + v[11]))
            total += (SHEAR / 8) * (square(u[100]) + square(v[10]) + square(z[1]))
            total += (SHEAR / 16) * (
                (square(u[110]) + square(u[101]) + square(v[110])) + (square(v[11]) + square(z[101]) + square(z[11]))
                + (square(u[10] + v[100]) + square(v[1] + z[10]) + square(u[1] + z[100])))
            total += (SHEAR / 48) * (square(u[11] + v[101]) + square(v[101] + z[110]) + square(u[11] + z[110]))
            total += ((LAME + 4 * SHEAR) / 144) * (square(u[111]) + square(v[111]) + square(z[111]))
            energy[pl.ds(pl.multiple_of((i - 1) * NY, NY) + 8 * t, 8), :] = total
            return now

        def pair(n, before):
            return tuple(element(2 * n + 2, element(2 * n + 1, before)))

        lax.fori_loop(first, end, pair, tuple(yz_terms(2 * first, t)))

    for t in range(NY // 8 - 1):
        energies(t, 0, NX // 2 - 1)
    wait_lower((-1, 0, 0), (-1, 0, -1))
    for n, v in enumerate(z_pass(ROWS, NY, [dxzr[m] for m in range(3)])):
        sd[n, pl.ds(NX * NODE_PAD, NY), :] = v
    for t in range(NY // 8 - 1):
        energies(t, NX // 2 - 1, NX // 2)
    add_xz(0, acc)
    wait_lower(*[d for d in LOWER if d[1]])
    for m in range(3):
        nodes[m, pl.ds(ROWS + NY + NX, 1), :] = dxyr[m]
    for n, v in enumerate(z_pass(ROWS + NY, NY, [pltpu.roll(dyzr[m] + dxyzr[m], 128 - NY, 1) for m in range(3)])):
        sd[n, pl.ds(NY, NX + 1, stride=NODE_PAD), :] = v[:NX + 1]
    energies(NY // 8 - 1, 0, NX // 2)

    def inverse_cover(index, extent):
        end = extent - 1
        return jnp.where(jnp.logical_or(index == 0, index == end), 1.0 / 6.0, jnp.where(
            jnp.logical_or(index == 1, index == end - 1), 1.0 / 8.0, 1.0 / 9.0)).astype(F32)

    inverse_yz = inverse_cover(iota((NY, NZ), 0) + gy * NY, NY * size_y) * inverse_cover(
        iota((NY, NZ), 1) + gz * NZ, NZ * size_z)

    def weigh(physical, energies_, inverse):
        product = physical * physical * energies_
        return -3.0 * product * inverse, physical * product

    y_rows = (0, 1, NY - 2, NY - 1)
    total = jnp.zeros((NY, NZ), F32)
    for i in range(NX):
        inverse = inverse_yz * inverse_cover(gx * NX + i, NX * size_x)
        slope, term = weigh(acc[pl.ds(i * NY, NY), :] * inverse, energy[pl.ds(i * NY, NY), :], inverse)
        field[pl.ds((i + 2) * NY, NY), :] = slope
        total = total + term
    row = iota((NY, NZ), 0)
    inner = jnp.logical_and(row >= 2, row < NY - 2)
    total = jnp.sum(jnp.where(inner, total, 0.0), axis=0, keepdims=True)

    inverse_x = inverse_cover(iota((NX, NZ), 0) + gx * NX, NX * size_x)
    inverses = [inverse_x * inverse_yz[row:row + 1] for row in y_rows]
    energy_rows = [energy[pl.ds(row, NX, stride=NY), :] for row in y_rows]
    add_y(0, acc)
    rows_total = jnp.zeros((NX, NZ), F32)
    for n, row in enumerate(y_rows):
        slope, term = weigh(acc[pl.ds(row, NX, stride=NY), :] * inverses[n], energy_rows[n], inverses[n])
        field[pl.ds(2 * NY + row, NX, stride=NY), :] = slope
        rows_total = rows_total + term
    total = total + jnp.sum(rows_total, axis=0, keepdims=True)

    def sum_copy(s, mine, to):
        return remote(part.at[s], part_in.at[s, mine], psend_sem.at[s], precv_sem.at[s], to)

    def sum_wait(sem, s, n):
        whole = part_in.at[s, pl.ds(0, n)]
        pltpu.make_async_copy(whole, whole, sem.at[s]).wait()

    mine = my_z * 2 + my_core
    part[0] = total
    for z, c in column:
        @pl.when(other(z, c))
        def _(z=z, c=c):
            sum_copy(0, mine, at_zc(z, c)).start()
    local_filter(1, out)
    for along_y in (1, 0, -1):
        send_filter(1, along_y)

    @pl.when(early)
    def _():
        part_in[0, mine] = total
        sum_wait(precv_sem, 0, 2 * count_z - 1)
        partial = jnp.sum(part_in[0, 0:2 * count_z], axis=0)
        here = gz * ring_y + my_y
        part[1] = partial
        part_in[1, here] = partial
        for o in plane:
            sum_copy(1, here, partner_xy(*o)).start()

    add_xz(1, out)
    add_y(1, out)

    for d in DIRECTIONS:
        @pl.when(inside(d))
        def _(d=d):
            for p in range(2):
                filter_copy(p, d).wait_send()
            if d in lower:
                lower_copy(d).wait_send()

    @pl.when(early)
    def _():
        sum_wait(psend_sem, 0, 2 * layers_z - 1)
        sum_wait(psend_sem, 1, len(plane))
        sum_wait(precv_sem, 1, len(plane))
        part[2] = jnp.sum(part_in[1, 0:len(plane) + 1], axis=0)

    def pass_on(z, c):
        return remote(
            part.at[2], part_in.at[2, 0], pass_sem.at[2 * (z - layers_z) + c], precv_sem.at[2], at_zc(z, c))

    for z, c in serves:
        @pl.when(serving(z))
        def _(z=z, c=c):
            pass_on(z, c).start()

    @pl.when(jnp.logical_not(early))
    def _():
        sum_wait(psend_sem, 0, 2 * layers_z)
        if halves > 1:
            sum_wait(precv_sem, 2, 1)
            part[2] = part_in[2, 0]

    total_out[...] = jnp.broadcast_to(jnp.sum(part[2], axis=1, keepdims=True), (8, 128))

    for z, c in serves:
        @pl.when(serving(z))
        def _(z=z, c=c):
            pass_on(z, c).wait_send()


def exchange(mesh, density, displacement):
    sizes = (mesh.shape["gx"], mesh.shape["gy"], mesh.shape["gz"], min(8, mesh.shape["gx"]))
    vmem = lambda *shape: pltpu.VMEM(shape, F32)
    partners = max(sizes[0] // sizes[3] * sizes[1], sizes[3] * sizes[2])
    scratch = [
        vmem((NX + 4) * NY, NZ), vmem(NX * YPAD, NZ), vmem(4 * YPAD, NZ), vmem(ROWS, NZ),
        vmem(128, NZ), vmem(128, NZ), vmem(3, ROWS + 2 * NY, NZ),
        vmem(6, 32 * NODE_PAD, NZ), vmem(ROWS, NZ)]
    filters = [vmem(2, 2, 2 * NY, NZ), vmem(2, 2, 2, NX, NZ), vmem(3, 2, 2, 4, 1, NZ), vmem(3, 2, 2 * GROUPS, 1, 128),
               vmem(3, 2, 2, 2, 1, 128), vmem(3, 2, 2, 2, 1, 128), vmem(3, 2, 2, 2, 2, 1, 128)]
    scratch += filters + filters
    edges = [vmem(11, 1, NZ), vmem(3 * GROUPS + 8, 1, 128), vmem(11, 1, 128), vmem(11, 1, 128), vmem(11, 1, 128)]
    scratch += [vmem(3, NX, NZ)] + edges + edges + [vmem(128, 128)]
    scratch += [vmem(11, 1, 128), vmem(4, partners, 1, 128)]
    dma = pltpu.SemaphoreType.DMA
    scratch += [dma((2, 27)), dma((2, 27)), dma((8,)), dma((8,)), dma((2,)), dma((3,)), dma((3,)), dma((8,))]
    return pl.pallas_call(
        functools.partial(kernel, sizes),
        out_shape=[jax.ShapeDtypeStruct((ROWS, NZ), F32), jax.ShapeDtypeStruct((8, 128), F32)],
        in_specs=[pl.BlockSpec(memory_space=pltpu.HBM)] * 2,
        out_specs=[pl.BlockSpec(memory_space=pltpu.VMEM)] * 2,
        scratch_shapes=scratch,
        compiler_params=pltpu.CompilerParams(
            collective_id=0, has_side_effects=True, vmem_limit_bytes=56_000_000),
        cost_estimate=pl.CostEstimate(flops=20_000_000, bytes_accessed=2_000_000, transcendentals=0),
    )(density, displacement)


def scale_kernel(elements, field, total, out, mean_out, scaled, mean_ref, sem):
    mean = total[0:1, :] / elements
    mean_ref[...] = mean[:, 0:1]
    inverse = 1.0 / mean
    copies = [pltpu.make_async_copy(mean_ref, mean_out, sem.at[PARTS])]
    copies[0].start()
    for n in range(PARTS):
        part = pl.ds(n * (ROWS // PARTS), ROWS // PARTS)
        scaled[part, :] = field[part, :] * inverse
        copies.append(pltpu.make_async_copy(scaled.at[part], out.at[part], sem.at[n]))
        copies[-1].start()
    for copy in copies:
        copy.wait()


def solution(mesh):
    def shards(displacement, density):
        filtered, total = exchange(mesh, density.reshape(ROWS, NZ), displacement.reshape(3, ROWS, NZ))
        sensitivity, mean = pl.pallas_call(
            functools.partial(scale_kernel, float(ROWS * NZ * mesh.size)),
            out_shape=[jax.ShapeDtypeStruct((ROWS, NZ), F32), jax.ShapeDtypeStruct((1, 1), F32)],
            in_specs=[pl.BlockSpec(memory_space=pltpu.VMEM)] * 2,
            out_specs=[pl.BlockSpec(memory_space=pl.ANY)] * 2,
            scratch_shapes=[
                pltpu.VMEM((ROWS, NZ), F32), pltpu.VMEM((1, 1), F32), pltpu.SemaphoreType.DMA((PARTS + 1,))],
            compiler_params=pltpu.CompilerParams(vmem_limit_bytes=4 * 2**20),
        )(filtered, total)
        return sensitivity.reshape(NX, NY, NZ), mean.reshape(())

    return jax.shard_map(
        shards,
        mesh=mesh,
        in_specs=(P(None, "gx", "gy", "gz"), P("gx", "gy", "gz")),
        out_specs=(P("gx", "gy", "gz"), P()),
        check_vma=False,
    )
```
